32 devices in a mesh: pipe: 4 (over y, core), expert: 8 (over z, x).
Axes of the slice: x: 2, y: 2, z: 4, core: 2. Of those that a mesh axis runs over, the one named last changes fastest.
Arguments:
- next_input: bfloat16 [4, 2048, 2048], P('pipe', 'expert'), may hold values from -6 to 6
- prev_input: bfloat16 [4, 2048, 2048], P('pipe', 'expert'), may hold values from -6 to 6
- next_cot: bfloat16 [4, 2048, 2048], P('pipe', 'expert'), may hold values from -6 to 6
- gate_weight: bfloat16 [4, 8, 2048, 768], P('pipe', 'expert'), may hold values from -0.125 to 0.125
- up_weight: bfloat16 [4, 8, 2048, 768], P('pipe', 'expert'), may hold values from -0.125 to 0.125
- down_weight: bfloat16 [4, 8, 768, 2048], P('pipe', 'expert'), may hold values from -0.21875 to 0.21875
- router: bfloat16 [4, 2048, 8], P('pipe'), may hold values from -0.125 to 0.125
- gain: float32 [4, 2048], P('pipe'), may hold values from 0.1 to 1.9
- next_routes: int32 [4, 2048, 2], P('pipe', 'expert'), may hold values from 0 to 7, all different within a row
- prev_routes: int32 [4, 2048, 2], P('pipe', 'expert'), may hold values from 0 to 7, all different within a row
- next_priority: int32 [4, 2048], P('pipe', 'expert'), may hold values from 0 to 2047, each once within a row
- prev_priority: int32 [4, 2048], P('pipe', 'expert'), may hold values from 0 to 2047, each once within a row
Outputs:
- forward_out: bfloat16 [4, 2048, 2048], P('pipe', 'expert')
- input_grad: bfloat16 [4, 2048, 2048], P('pipe', 'expert')
- gate_grad: bfloat16 [4, 8, 2048, 768], P('pipe', 'expert')
- up_grad: bfloat16 [4, 8, 2048, 768], P('pipe', 'expert')
- down_grad: bfloat16 [4, 8, 768, 2048], P('pipe', 'expert')
- router_grad: float32 [4, 2048, 8], P('pipe')
- gain_grad: float32 [4, 2048], P('pipe')
The draws below stay inside these ranges and needn't reach their ends.
All inputs are finite; a program needn't handle non-finite values.
Results may differ from the reference program's by a relative error of at most 0.0085.
Values may be sent and summed in bfloat16 or wider, within the bound.
No kernel may reach another device: no remote copies, remote signals or barrier semaphores. Data moves between devices by JAX's collectives and lax.ppermute only.
A program may use at most 128 MiB of HBM per device.

```python
import jax
import jax.numpy as jnp
from jax import lax

D = 2048
FF = 768
TOP = 2
TOK_DEV = 256
EXPERTS = 8
TOKENS = 2048
CAP = 80
N_PIPE = 4
N_EXPERT = 8


def steps_of(key, extent, split, least, top_value):
    level, own = 1.0, jax.random.fold_in(key, 6)
    for position, shards_of in split:
        draws = jnp.exp(jax.random.uniform(jax.random.fold_in(own, position), (shards_of,), jnp.float32, least / len(split), top_value / len(split)))
        level = level * jnp.repeat(draws, extent[position] // shards_of).reshape([-1 if axis == position else 1 for axis in range(len(extent))])
    return level


def different_ones(own_key, rows, amount, top, lift):
    ranking = jax.random.permutation(jax.random.fold_in(own_key, 1), amount)
    boost = ranking
    for power in range(3):
        boost = boost * boost // amount
    boost = boost * lift // amount
    lots = jax.random.randint(jax.random.fold_in(own_key, 2), (rows, amount), 0, 4096) + boost
    sure = jax.random.permutation(jax.random.fold_in(own_key, 3), rows)[jnp.arange(amount) % rows]
    lots = jnp.where(jnp.arange(rows)[:, None] == sure[None, :], 1 << 14, lots)
    score = lots * amount + jnp.arange(amount)
    return lax.top_k(score.astype(jnp.int32), top)[1].astype(jnp.int32)


def noise(own_key, extent, scale, limit, pieces=(), held_as=jnp.bfloat16):
    values = jax.random.normal(own_key, extent, jnp.float32) * scale
    if len(pieces) > 0:
        values = steps_of(own_key, extent, pieces, -0.22, 0.18) * values
    return jnp.clip(values, min=-limit, max=limit).astype(held_as)


def setup_inputs(seed: int = 0) -> dict:
    keys = jax.random.split(jax.random.key(seed), 13)
    return {
        "next_input": noise(keys[0], (N_PIPE, TOKENS, D), 1.0, 6.0, ((0, 4), (1, 8))),
        "prev_input": noise(keys[1], (N_PIPE, TOKENS, D), 1.0, 6.0, ((0, 4), (1, 8))),
        "next_cot": noise(keys[2], (N_PIPE, TOKENS, D), 1.0, 6.0, ((0, 4), (1, 8))),
        "gate_weight": noise(keys[3], (N_PIPE, EXPERTS, D, FF), D ** -0.5, 0.125, ((0, 4), (1, 8))),
        "up_weight": noise(keys[4], (N_PIPE, EXPERTS, D, FF), D ** -0.5, 0.125, ((0, 4), (1, 8))),
        "down_weight": noise(keys[5], (N_PIPE, EXPERTS, FF, D), FF ** -0.5, 0.21875, ((0, 4), (1, 8))),
        "router": noise(keys[6], (N_PIPE, D, EXPERTS), D ** -0.5, 0.125, ((0, 4),)),
        "gain": jnp.clip(1.0 + 0.18 * jax.random.normal(keys[7], (N_PIPE, D), jnp.float32), 0.1, 1.9),
        "next_routes": different_ones(keys[8], N_PIPE * TOKENS, EXPERTS, TOP, 4096).reshape((N_PIPE, TOKENS, TOP)),
        "prev_routes": different_ones(keys[9], N_PIPE * TOKENS, EXPERTS, TOP, 4096).reshape((N_PIPE, TOKENS, TOP)),
        "next_priority": jax.vmap(lambda own: jax.random.permutation(own, TOKENS))(jax.random.split(keys[10], N_PIPE)).reshape((N_PIPE, TOKENS)).astype(jnp.int32),
        "prev_priority": jax.vmap(lambda own: jax.random.permutation(own, TOKENS))(jax.random.split(keys[11], N_PIPE)).reshape((N_PIPE, TOKENS)).astype(jnp.int32),
    }


EPS = 1e-06

def rms_scaled(values, gain):
    scale = lax.rsqrt(lax.optimization_barrier(jnp.mean(values * values, axis=-1, keepdims=True)) + EPS)
    return values * scale * gain

def pair_weights(selected):
    lifted = jax.nn.sigmoid(selected)
    return lifted / lax.optimization_barrier(jnp.sum(lifted, axis=-1, keepdims=True))

def slot_table(routes, priority, experts, capacity):
    top = routes.shape[1]
    picks = routes.reshape(-1).astype(jnp.int32)
    order = jnp.repeat(priority, top)
    same = picks[:, None] == picks[None, :]
    before = order[None, :] < order[:, None]
    rank = lax.optimization_barrier(jnp.sum(jnp.where(same & before, 1, 0), axis=1)).astype(jnp.int32)
    kept = rank < capacity
    slots = jnp.where(kept, picks * capacity + rank, experts * capacity).astype(jnp.int32)
    match = slots[None, :] == jnp.arange(experts * capacity, dtype=jnp.int32)[:, None]
    filled = jnp.any(match, axis=1)
    source = lax.optimization_barrier(jnp.sum(jnp.where(match, jnp.arange(picks.shape[0], dtype=jnp.int32)[None, :], 0), axis=1)).astype(jnp.int32)
    return (slots, filled, source)

def prepare(section_in, gain, router, routes, priority, capacity):
    experts = router.shape[-1]
    top = routes.shape[1]
    values = section_in.astype(jnp.float32)
    normed = rms_scaled(values, gain).astype(jnp.bfloat16)
    logits = jnp.dot(normed.astype(jnp.float32), router.astype(jnp.float32), preferred_element_type=jnp.float32)
    selected = jnp.take_along_axis(logits, routes, axis=1)
    slots, filled, source = slot_table(routes, priority, experts, capacity)
    token = source // top
    rows = jnp.where(filled[:, None], normed[token], jnp.zeros_like(normed[token]))
    rows = rows.reshape(experts, capacity, normed.shape[1])
    return (values, normed, selected, slots, filled, source, rows)

def pick_rows(table, slots):
    flat = table.reshape(-1, table.shape[-1])
    padded = jnp.concatenate([flat, jnp.zeros((1, flat.shape[1]), flat.dtype)], axis=0)
    return padded[slots].astype(jnp.float32)

def combine(values, selected, slots, produced):
    top = selected.shape[1]
    weights = pair_weights(selected).reshape(-1, 1)
    taken = pick_rows(produced, slots) * weights
    total = lax.optimization_barrier(jnp.sum(taken.reshape(values.shape[0], top, values.shape[1]), axis=1))
    return (values + total).astype(jnp.bfloat16)

def as_wide(array):
    return array.astype(jnp.float32)

def expert_forward(shaped, gate_w, up_w, down_w):
    gate = jnp.einsum('secd,edf->secf', as_wide(shaped), as_wide(gate_w))
    upper = jnp.einsum('secd,edf->secf', as_wide(shaped), as_wide(up_w))
    active = (gate * jax.nn.sigmoid(gate) * upper).astype(jnp.bfloat16)
    return jnp.einsum('secf,efd->secd', as_wide(active), as_wide(down_w)).astype(jnp.bfloat16)

def expert_backward(shaped, cot, scales, gate_w, up_w, down_w):
    gate = jnp.einsum('secd,edf->secf', as_wide(shaped), as_wide(gate_w))
    upper = jnp.einsum('secd,edf->secf', as_wide(shaped), as_wide(up_w))
    sig = jax.nn.sigmoid(gate)
    lifted = gate * sig
    active = (lifted * upper).astype(jnp.bfloat16)
    result = jnp.einsum('secf,efd->secd', as_wide(active), as_wide(down_w)).astype(jnp.bfloat16)
    inner = lax.optimization_barrier(jnp.sum(cot.astype(jnp.float32) * result.astype(jnp.float32), axis=-1, keepdims=True)).astype(jnp.bfloat16)
    scaled = (scales.astype(jnp.float32) * cot.astype(jnp.float32)).astype(jnp.bfloat16)
    down_part = jnp.einsum('secf,secd->efd', as_wide(active), as_wide(scaled))
    act_grad = jnp.einsum('secd,efd->secf', as_wide(scaled), as_wide(down_w))
    gate_part = (act_grad * upper * sig * (1.0 + gate * (1.0 - sig))).astype(jnp.bfloat16)
    up_part = (act_grad * lifted).astype(jnp.bfloat16)
    gate_wgrad = jnp.einsum('secd,secf->edf', as_wide(shaped), as_wide(gate_part))
    up_wgrad = jnp.einsum('secd,secf->edf', as_wide(shaped), as_wide(up_part))
    row_grad = jnp.einsum('secf,edf->secd', as_wide(gate_part), as_wide(gate_w))
    row_grad = (row_grad + jnp.einsum('secf,edf->secd', as_wide(up_part), as_wide(up_w))).astype(jnp.bfloat16)
    return (row_grad, inner, gate_wgrad, up_wgrad, down_part)

def slot_scales(selected, filled, source):
    flat = pair_weights(selected).reshape(-1)
    return jnp.where(filled, flat[source], 0.0).astype(jnp.bfloat16)

def source_backward(values, normed, selected, routes, gain, router, slots, row_grad, inner, cot_in):
    top = routes.shape[1]
    experts = router.shape[-1]
    width = values.shape[1]
    pulled = pick_rows(row_grad, slots).reshape(values.shape[0], top, width)
    dnormed = lax.optimization_barrier(jnp.sum(pulled, axis=1))
    dweight = pick_rows(inner, slots).reshape(values.shape[0], top)
    _, pull = jax.vjp(pair_weights, selected)
    dsel = pull(dweight)[0]
    onehot = (routes[:, :, None] == jnp.arange(experts, dtype=jnp.int32)[None, None, :]).astype(jnp.float32)
    dlogits = lax.optimization_barrier(jnp.sum(onehot * dsel[:, :, None], axis=1))
    router_f = router.astype(jnp.float32)
    dnormed = dnormed + jnp.dot(dlogits, router_f.T, precision=lax.Precision.HIGHEST)
    router_part = jnp.dot(normed.astype(jnp.float32).T, dlogits, precision=lax.Precision.HIGHEST)
    _, pull_norm = jax.vjp(rms_scaled, values, gain)
    dvalues, dgain = pull_norm(dnormed)
    grad_in = (cot_in.astype(jnp.float32) + dvalues).astype(jnp.bfloat16)
    return (grad_in, router_part, dgain)

def reference(next_input, prev_input, next_cot, gate_weight, up_weight, down_weight, router, gain, next_routes, prev_routes, next_priority, prev_priority):
    capacity = CAP
    blocks = N_EXPERT
    section_in = jnp.roll(next_input, 1, axis=0)
    cot_all = jnp.roll(next_cot, -1, axis=0)
    outs = ([], [], [], [], [], [], [])
    for section in range(N_PIPE):
        gw, uw, dw = (gate_weight[section], up_weight[section], down_weight[section])
        rw, gn = (router[section], gain[section])

        def prep(x_blk, r_blk, p_blk):
            return prepare(x_blk, gn, rw, r_blk, p_blk, capacity)
        xs = section_in[section].reshape(blocks, TOK_DEV, D)
        values, normed, selected, slots, filled, source, rows = jax.vmap(prep)(xs, next_routes[section].reshape(blocks, TOK_DEV, TOP), next_priority[section].reshape(blocks, TOK_DEV))
        produced = expert_forward(rows, gw, uw, dw)
        forward = jax.vmap(combine)(values, selected, slots, produced)
        outs[0].append(forward.reshape(TOKENS, D))
        xp = prev_input[section].reshape(blocks, TOK_DEV, D)
        proutes = prev_routes[section].reshape(blocks, TOK_DEV, TOP)
        values, normed, selected, slots, filled, source, rows = jax.vmap(prep)(xp, proutes, prev_priority[section].reshape(blocks, TOK_DEV))
        cot_in = cot_all[section].reshape(blocks, TOK_DEV, D)
        token = source // TOP
        cot_rows = jax.vmap(lambda c, f, t: jnp.where(f[:, None], c[t], jnp.zeros_like(c[t])))(cot_in, filled, token)
        cot_rows = cot_rows.reshape(rows.shape)
        scales = jax.vmap(slot_scales)(selected, filled, source).reshape(rows.shape[:3] + (1,))
        row_grad, inner, gate_wgrad, up_wgrad, down_part = expert_backward(rows, cot_rows, scales, gw, uw, dw)

        def finish(v, n, s, r, sl, rg, inn, c):
            return source_backward(v, n, s, r, gn, rw, sl, rg, inn, c)
        grad_in, router_part, dgain = jax.vmap(finish)(values, normed, selected, proutes, slots, row_grad, inner, cot_in)
        outs[1].append(grad_in.reshape(TOKENS, D))
        outs[2].append(gate_wgrad.astype(jnp.bfloat16))
        outs[3].append(up_wgrad.astype(jnp.bfloat16))
        outs[4].append(down_part.astype(jnp.bfloat16))
        outs[5].append(lax.optimization_barrier(jnp.sum(router_part, axis=0)))
        outs[6].append(lax.optimization_barrier(jnp.sum(dgain, axis=0)))
    return (jnp.stack(outs[0]), jnp.stack(outs[1]), jnp.stack(outs[2]), jnp.stack(outs[3]), jnp.stack(outs[4]), jnp.stack(outs[5]), jnp.stack(outs[6]))
```

```python
import jax
import jax.numpy as jnp
from jax import lax
from jax.sharding import PartitionSpec as P

EPS = 1e-06
F32 = jnp.float32
BF16 = jnp.bfloat16


def rms_scaled(values, gain):
    scale = lax.rsqrt(jnp.mean(values * values, axis=-1, keepdims=True) + EPS)
    return values * scale * gain


def hop(block, pipe_step, flip):
    pipes, experts = lax.axis_size("pipe"), lax.axis_size("expert")
    if pipe_step == 0:
        return lax.ppermute(block, "expert", [(e, e ^ flip) for e in range(experts)])
    route = [
        (p * experts + e, ((p + pipe_step) % pipes) * experts + (e ^ flip))
        for p in range(pipes)
        for e in range(experts)
    ]
    return lax.ppermute(block, ("pipe", "expert"), route)


def exchange(pieces):
    return [piece if k == 0 else hop(piece, 0, k) for k, piece in enumerate(pieces)]


def after(block, *earlier):
    return lax.optimization_barrier((block,) + earlier)[0]


def routing(routes, priority, wanted):
    before = (priority[:, None] < priority[None, :]).astype(BF16)
    chosen = jnp.any(routes[None, :, :] == wanted[:, None, None], axis=1)
    count = jnp.dot(chosen.astype(BF16), before, preferred_element_type=F32)
    return jnp.where(chosen, count.astype(jnp.int32), -1)


def slots_of(rank, capacity):
    place = lax.broadcasted_iota(jnp.int32, (rank.shape[0], capacity, rank.shape[1]), 1)
    return place == rank[:, None, :]


def gate_of(normed, router, routes, wanted):
    logits = lax.dot_general(
        router, normed, (((0,), (1,)), ((), ())), preferred_element_type=F32
    )
    experts = jnp.arange(logits.shape[0], dtype=jnp.int32)
    pick = routes[:, None, :] == experts[None, :, None]
    lifted = jax.nn.sigmoid(jnp.sum(jnp.where(pick, logits[None], 0.0), axis=1))
    weight = lifted / jnp.sum(lifted, axis=0, keepdims=True)
    at = routes[None, :, :] == wanted[:, None, None]
    return lifted, jnp.sum(jnp.where(at, weight[None], 0.0), axis=1)


def slot_rows(slots, block):
    return [jnp.dot(s.astype(BF16), block, preferred_element_type=F32).astype(BF16) for s in slots]


def tokens_of(slots, weight, produced):
    table = jnp.concatenate(produced, axis=0)
    dims = (((0,), (0,)), ((), ()))
    if weight is None:
        spread = slots.astype(BF16).reshape(table.shape[0], -1)
        return lax.dot_general(spread, table, dims, preferred_element_type=F32)
    spread = jnp.where(slots, weight[:, None, :], 0.0).reshape(table.shape[0], -1)
    high = spread.astype(BF16)
    low = (spread - high.astype(F32)).astype(BF16)
    total = lax.dot_general(high, table, dims, preferred_element_type=F32)
    return total + lax.dot_general(low, table, dims, preferred_element_type=F32)


def per_device(
    next_input,
    prev_input,
    next_cot,
    gate_weight,
    up_weight,
    down_weight,
    router,
    gain,
    next_routes,
    prev_routes,
    next_priority,
    prev_priority,
):
    experts = router.shape[-1]
    tokens, width = next_input.shape[1:]
    top = next_routes.shape[-1]
    capacity = (5 * top * tokens + 4 * experts - 1) // (4 * experts)
    gate_w, up_w, down_w = (gate_weight[0, 0], up_weight[0, 0], down_weight[0, 0])
    router_w, gain_v = (router[0], gain[0])
    half = lax.axis_size("expert") // 2
    me = lax.axis_index("expert")
    wanted = me ^ jnp.arange(half, dtype=jnp.int32)

    tables = jnp.concatenate(
        [next_routes[0].T, prev_routes[0].T, next_priority, prev_priority], axis=0
    )
    far_tables = hop(tables, 0, half)
    xp_own = prev_input[0]
    xp_far = hop(xp_own, 0, half)
    dy_own = hop(next_cot[0], -1, 0)
    x_own = hop(next_input[0], 1, 0)
    dy_far = hop(after(next_cot[0], xp_far), -1, half)
    x_far = hop(after(next_input[0], dy_far), 1, half)

    def split_tables(packed):
        return (
            (packed[:top], packed[2 * top]),
            (packed[top : 2 * top], packed[2 * top + 1]),
        )

    (fwd_own, bwd_own), (fwd_far, bwd_far) = split_tables(tables), split_tables(far_tables)

    def prepare(block, where):
        routes, priority = where
        normed = rms_scaled(block.astype(F32), gain_v).astype(BF16)
        slots = slots_of(routing(routes, priority, wanted), capacity)
        lifted, weight = gate_of(normed, router_w, routes, wanted)
        return normed, slots, lifted, weight

    def slot_weights(slots, weight):
        rounded = weight.astype(BF16).astype(F32)
        return jnp.sum(jnp.where(slots, rounded[:, None, :], 0.0), axis=2)

    normed, slots_own, lifted, weight_own = prepare(xp_own, bwd_own)
    rows_own = exchange(slot_rows(slots_own, normed))
    normed_far, slots_far, _, weight_far = prepare(xp_far, bwd_far)
    rows_far = exchange(slot_rows(slots_far, normed_far))
    scale_own = slot_weights(slots_own, weight_own)
    scale_far = slot_weights(slots_far, weight_far)
    scales = exchange([jnp.concatenate([scale_own[k], scale_far[k]]) for k in range(half)])
    scales = jnp.stack(scales).reshape(half, 2, capacity).swapaxes(0, 1).reshape(-1, 1)
    cot_own = exchange(slot_rows(slots_own, dy_own))
    cot_far = exchange(slot_rows(slots_far, dy_far))

    _, fslots_own, _, fweight_own = prepare(x_own, fwd_own)
    normed_f = rms_scaled(x_own.astype(F32), gain_v).astype(BF16)
    frows_own = exchange(slot_rows(fslots_own, normed_f))
    normed_ff, fslots_far, _, fweight_far = prepare(x_far, fwd_far)
    frows_far = exchange(slot_rows(fslots_far, normed_ff))

    flat = jnp.concatenate(rows_own + rows_far, axis=0)
    cot = jnp.concatenate(cot_own + cot_far, axis=0)
    gate = jnp.dot(flat, gate_w, preferred_element_type=F32)
    upper = jnp.dot(flat, up_w, preferred_element_type=F32)
    sig = jax.nn.sigmoid(gate)
    act = gate * sig
    active = (act * upper).astype(BF16)
    result = jnp.dot(active, down_w, preferred_element_type=F32).astype(BF16)
    inner = jnp.sum(cot.astype(F32) * result.astype(F32), axis=-1).astype(BF16)
    scaled = (scales * cot.astype(F32)).astype(BF16)
    act_grad = lax.dot_general(scaled, down_w, (((1,), (1,)), ((), ())), preferred_element_type=F32)
    gate_part = (act_grad * upper * sig * (1.0 + gate * (1.0 - sig))).astype(BF16)
    up_part = (act_grad * act).astype(BF16)
    dims = (((1,), (1,)), ((), ()))
    row_grad = lax.dot_general(gate_part, gate_w, dims, preferred_element_type=F32)
    row_grad = row_grad + lax.dot_general(up_part, up_w, dims, preferred_element_type=F32)
    row_grad = row_grad.astype(BF16).reshape(2, half, capacity, width)
    dims = (((0,), (0,)), ((), ()))
    gate_wgrad = lax.dot_general(flat, gate_part, dims, preferred_element_type=F32).astype(BF16)
    up_wgrad = lax.dot_general(flat, up_part, dims, preferred_element_type=F32).astype(BF16)
    down_wgrad = lax.dot_general(active, scaled, dims, preferred_element_type=F32).astype(BF16)

    inner = inner.astype(F32).reshape(2, half, capacity)
    inner = exchange([inner[:, k].reshape(-1) for k in range(half)])
    inner = jnp.stack(inner).reshape(half, 2, capacity)
    grads_far = tokens_of(slots_far, None, exchange([row_grad[1, k] for k in range(half)]))
    grads_cross = hop(grads_far.astype(BF16), 0, half)
    grads_own = tokens_of(slots_own, None, exchange([row_grad[0, k] for k in range(half)]))

    def weight_terms(slots, part):
        return jnp.sum(jnp.where(slots, part[:, :, None], 0.0), axis=1)

    routes_own = bwd_own[0]
    far_terms = hop(weight_terms(slots_far, inner[:, 1]), 0, half)
    own_terms = weight_terms(slots_own, inner[:, 0])
    at = routes_own[None, :, :] == wanted[:, None, None]
    dweight = jnp.sum(jnp.where(at, own_terms[:, None, :], 0.0), axis=0)
    far_at = routes_own[None, :, :] == (wanted ^ half)[:, None, None]
    dweight = dweight + jnp.sum(jnp.where(far_at, far_terms[:, None, :], 0.0), axis=0)

    def forward_part(pieces):
        flat = jnp.concatenate(pieces, axis=0)
        gate = jnp.dot(flat, gate_w, preferred_element_type=F32)
        upper = jnp.dot(flat, up_w, preferred_element_type=F32)
        active = (gate * jax.nn.sigmoid(gate) * upper).astype(BF16)
        result = jnp.dot(active, down_w, preferred_element_type=F32).astype(BF16)
        result = result.reshape(half, capacity, width)
        return exchange([result[k] for k in range(half)])

    out_own = forward_part(frows_own)
    out_far = forward_part(frows_far)
    sum_far = tokens_of(fslots_far, fweight_far, out_far)
    sum_cross = hop(after(sum_far.astype(BF16), grads_cross), 0, half)
    sum_own = tokens_of(fslots_own, fweight_own, out_own)

    total = jnp.sum(lifted, axis=0, keepdims=True)
    dlifted = dweight / total - jnp.sum(dweight * lifted, axis=0, keepdims=True) / (total * total)
    dsel = dlifted * lifted * (1.0 - lifted)
    everyone = jnp.arange(experts, dtype=jnp.int32)
    pick = routes_own[:, None, :] == everyone[None, :, None]
    dlogits = jnp.sum(jnp.where(pick, dsel[:, None, :], 0.0), axis=0)
    dims = (((0,), (1,)), ((), ()))
    dnormed = grads_own + grads_cross.astype(F32)
    dnormed = dnormed + lax.dot_general(
        dlogits, router_w.astype(F32), dims, precision=lax.Precision.HIGHEST
    )
    router_part = jnp.dot(dlogits, normed.astype(F32), precision=lax.Precision.HIGHEST)
    values = xp_own.astype(F32)
    _, pull_norm = jax.vjp(rms_scaled, values, gain_v)
    dvalues, dgain = pull_norm(dnormed)
    grad_in = (dy_own.astype(F32) + dvalues).astype(BF16)
    sums = jnp.concatenate([router_part, dgain[None]], axis=0)
    sums = jnp.pad(sums, ((0, -sums.shape[0] % 8), (0, 0)))
    step = 1
    while step < lax.axis_size("expert"):
        sums = sums + hop(sums, 0, step)
        step *= 2

    forward = (x_own.astype(F32) + sum_own + sum_cross.astype(F32)).astype(BF16)
    return (
        forward[None],
        grad_in[None],
        gate_wgrad[None, None],
        up_wgrad[None, None],
        down_wgrad[None, None],
        sums[:experts].T[None],
        sums[experts][None],
    )


def solution(mesh):
    rows = P("pipe", "expert", None)
    weights = P("pipe", "expert", None, None)
    shared = P("pipe", None, None)
    return jax.shard_map(
        per_device,
        mesh=mesh,
        in_specs=(rows,) * 3
        + (weights,) * 3
        + (shared, P("pipe", None), rows, rows, P("pipe", "expert"), P("pipe", "expert")),
        out_specs=(rows, rows, weights, weights, weights, shared, P("pipe", None)),
        check_vma=False,
    )
```

```python
import functools

import jax
import jax.numpy as jnp
from jax import lax
from jax.experimental import pallas as pl
from jax.experimental.pallas import tpu as pltpu
from jax.sharding import PartitionSpec as P

EPS = 1e-06
F32 = jnp.float32
BF16 = jnp.bfloat16
VMEM_BYTES = 48 * 1024 * 1024


def hop(block, pipe_step, flip, name):
    pipes, experts = lax.axis_size("pipe"), lax.axis_size("expert")
    with jax.named_scope(name):
        if pipe_step == 0:
            return lax.ppermute(block, "expert", [(e, e ^ flip) for e in range(experts)])
        route = [
            (p * experts + e, ((p + pipe_step) % pipes) * experts + (e ^ flip))
            for p in range(pipes)
            for e in range(experts)
        ]
        return lax.ppermute(block, ("pipe", "expert"), route)


def exchange(pieces, name):
    return [piece if k == 0 else hop(piece, 0, k, name) for k, piece in enumerate(pieces)]


def after(block, *earlier):
    return lax.optimization_barrier((block,) + earlier)[0]


def dot(a, b):
    return jnp.dot(a, b, preferred_element_type=F32)


def dot_t(a, b):
    return lax.dot_general(a, b, (((1,), (1,)), ((), ())), preferred_element_type=F32)


def t_dot(a, b, precision=None):
    dims = (((0,), (0,)), ((), ()))
    return lax.dot_general(a, b, dims, preferred_element_type=F32, precision=precision)


def iota(shape, dim):
    return lax.broadcasted_iota(jnp.int32, shape, dim)


def call(kernel, name, outs, ins, grid=(), in_specs=None, out_specs=None, scratch=(), flops=0):
    whole = pl.BlockSpec(memory_space=pltpu.VMEM)
    moved = sum(a.size * a.dtype.itemsize for a in list(outs) + list(ins))
    return pl.pallas_call(
        kernel,
        out_shape=[jax.ShapeDtypeStruct(o.shape, o.dtype) for o in outs],
        grid=grid,
        in_specs=in_specs or [whole] * len(ins),
        out_specs=out_specs or [whole] * len(outs),
        scratch_shapes=list(scratch),
        compiler_params=pltpu.CompilerParams(vmem_limit_bytes=VMEM_BYTES),
        cost_estimate=pl.CostEstimate(flops=flops, bytes_accessed=moved, transcendentals=0),
        name=name,
    )(*ins)


def shape(dims, dtype=BF16):
    return jax.ShapeDtypeStruct(tuple(dims), dtype)


def rank_kernel(capacity, half, top, me_ref, own_ref, far_ref, *rank_refs):
    tokens = own_ref.shape[1]
    wanted = me_ref[0] ^ iota((half, tokens), 0)
    outs = iter(rank_refs)
    for ref in (own_ref, far_ref):
        for batch in range(2):
            order = jnp.broadcast_to(ref[2 * top + batch : 2 * top + batch + 1, :], (tokens, tokens))
            before = (order.T < order).astype(F32).astype(BF16)
            chosen = iota((half, tokens), 0) < 0
            for j in range(top):
                row = batch * top + j
                chosen = chosen | (ref[row : row + 1, :] == wanted)
            count = dot(chosen.astype(F32).astype(BF16), before)
            next(outs)[...] = jnp.where(chosen & (count < capacity), count.astype(jnp.int32), -1)


def slot_mask(rank_ref, k, slots):
    rank = rank_ref[k : k + 1, :]
    return iota((slots, rank.shape[1]), 0) == rank


def one_hot(mask):
    return jnp.where(mask, 1.0, 0.0).astype(BF16)


def normalise(x_ref, gain_ref, normed_ref, step=32):
    def part(i, carry):
        rows = pl.ds(pl.multiple_of(i * step, step), step)
        values = x_ref[rows, :].astype(F32)
        scale = lax.rsqrt(jnp.mean(values * values, axis=-1, keepdims=True) + EPS)
        normed_ref[rows, :] = (values * scale * gain_ref[...]).astype(BF16)
        return carry

    lax.fori_loop(0, x_ref.shape[0] // step, part, 0)


def gates(me, normed_ref, router_ref, routes, lifted_ref, weight_ref):
    logits = dot_t(router_ref[...], normed_ref[...])
    everyone = iota(logits.shape, 0)
    lifted = [
        jax.nn.sigmoid(jnp.sum(jnp.where(r == everyone, logits, 0.0), axis=0, keepdims=True))
        for r in routes
    ]
    total = functools.reduce(jnp.add, lifted)
    wanted = me ^ iota(weight_ref.shape, 0)
    weight = jnp.zeros(weight_ref.shape, F32)
    for j, (r, value) in enumerate(zip(routes, lifted)):
        if lifted_ref is not None:
            lifted_ref[j : j + 1, :] = value
        weight = weight + jnp.where(r == wanted, value / total, 0.0)
    weight_ref[...] = weight


def slot_scales(rank_ref, weight_ref, scale_ref):
    for k in range(rank_ref.shape[0]):
        mask = slot_mask(rank_ref, k, scale_ref.shape[1])
        weight = jnp.broadcast_to(weight_ref[k : k + 1, :].astype(BF16), (16, mask.shape[1]))
        scale_ref[k : k + 1, :] = dot_t(weight, one_hot(mask))[:1, :]


def route_rows(ref, batch, top):
    return [ref[batch * top + j : batch * top + j + 1, :] for j in range(top)]


def own_kernel(half, top, *refs):
    (me_ref, xp_ref, dy_ref, x_ref, gain_ref, router_ref, table_ref, frank_ref, rank_ref) = refs[:9]
    pieces = refs[9 : 9 + half]
    normed_ref, lifted_ref, weight_ref, scale_ref, fweight_ref, fnormed = refs[9 + half :]
    slots = pieces[0].shape[1]
    normalise(xp_ref, gain_ref, normed_ref)
    normalise(x_ref, gain_ref, fnormed)
    for k in range(half):
        hot = one_hot(slot_mask(rank_ref, k, slots))
        pieces[k][0] = dot(hot, normed_ref[...]).astype(BF16)
        pieces[k][1] = dot(hot, dy_ref[...]).astype(BF16)
        hot = one_hot(slot_mask(frank_ref, k, slots))
        pieces[k][2] = dot(hot, fnormed[...]).astype(BF16)
    me = me_ref[0]
    gates(me, normed_ref, router_ref, route_rows(table_ref, 1, top), lifted_ref, weight_ref)
    slot_scales(rank_ref, weight_ref, scale_ref)
    gates(me, fnormed, router_ref, route_rows(table_ref, 0, top), None, fweight_ref)


def far_kernel(half, top, batch, *refs):
    (me_ref, x_ref, gain_ref, router_ref, table_ref, rank_ref) = refs[:6]
    pieces = refs[6 : 6 + half]
    weight_ref, scale_ref, normed = refs[6 + half :]
    normalise(x_ref, gain_ref, normed)
    for k in range(half):
        hot = one_hot(slot_mask(rank_ref, k, pieces[0].shape[0]))
        pieces[k][...] = dot(hot, normed[...]).astype(BF16)
    routes = route_rows(table_ref, batch, top)
    gates(me_ref[0], normed, router_ref, routes, None, weight_ref)
    slot_scales(rank_ref, weight_ref, scale_ref)


def plain_kernel(rank_ref, x_ref, *pieces):
    for k, piece in enumerate(pieces):
        hot = one_hot(slot_mask(rank_ref, k, piece.shape[0]))
        piece[...] = dot(hot, x_ref[...]).astype(BF16)


def gather_flat(refs, flat_ref):
    at = 0
    for ref in refs:
        value = ref[...].reshape(ref.shape[-2:])
        flat_ref[at : at + value.shape[0], :] = value
        at += value.shape[0]


def hidden_kernel(count, *refs):
    rows = refs[:count]
    gate_w, up_w, down_w, flat, gate_ref, upper_ref, active_ref, result_ref, acc = refs[count:]
    step = pl.program_id(0)

    @pl.when(step == 0)
    def _():
        gather_flat(rows, flat)
        acc[...] = jnp.zeros_like(acc)

    gate = dot(flat[...], gate_w[...])
    upper = dot(flat[...], up_w[...])
    active = (gate * jax.nn.sigmoid(gate) * upper).astype(BF16)
    gate_ref[...] = gate
    upper_ref[...] = upper
    active_ref[...] = active
    acc[...] += dot(active, down_w[...])

    @pl.when(step == pl.num_programs(0) - 1)
    def _():
        result_ref[...] = acc[...].astype(BF16)


def back_kernel(count, half, *refs):
    cots = refs[:count]
    scale_refs, refs = refs[count : count + half], refs[count + half :]
    gate_w, up_w, down_w, gate_ref, upper_ref, result_ref = refs[:6]
    grads, inners = refs[6 : 6 + count], refs[6 + count : 6 + count + half]
    scaled_ref, gate_part_ref, up_part_ref, acc = refs[6 + count + half :]
    step = pl.program_id(0)
    slots = grads[0].shape[0]

    @pl.when(step == 0)
    def _():
        eye = iota((slots, slots), 0) == iota((slots, slots), 1)
        for i, ref in enumerate(cots):
            k, b = i % half, i // half
            rows = slice(i * slots, (i + 1) * slots)
            cot = ref[...].reshape(ref.shape[-2:]).astype(F32)
            scale = jnp.sum(jnp.where(eye, scale_refs[k][b : b + 1, :], 0.0), axis=1, keepdims=True)
            scaled_ref[rows, :] = (scale * cot).astype(BF16)
            inner = jnp.sum(cot * result_ref[rows, :].astype(F32), axis=1, keepdims=True)
            inner = jnp.sum(jnp.where(eye, inner, 0.0), axis=0, keepdims=True)
            inners[k][b : b + 1, :] = inner.astype(BF16).astype(F32)
        acc[...] = jnp.zeros_like(acc)

    act_grad = dot_t(scaled_ref[...], down_w[...])
    gate = gate_ref[...]
    sig = jax.nn.sigmoid(gate)
    gate_part = (act_grad * upper_ref[...] * sig * (1.0 + gate * (1.0 - sig))).astype(BF16)
    up_part = (act_grad * (gate * sig)).astype(BF16)
    gate_part_ref[...] = gate_part
    up_part_ref[...] = up_part
    acc[...] += dot_t(gate_part, gate_w[...]) + dot_t(up_part, up_w[...])

    @pl.when(step == pl.num_programs(0) - 1)
    def _():
        for i, ref in enumerate(grads):
            ref[...] = acc[i * slots : (i + 1) * slots, :].astype(BF16)


def forward_kernel(count, *refs):
    rows = refs[:count]
    gate_w, up_w, down_w = refs[count : count + 3]
    outs, (flat, acc) = refs[count + 3 : 2 * count + 3], refs[2 * count + 3 :]
    step = pl.program_id(0)
    slots = outs[0].shape[0]

    @pl.when(step == 0)
    def _():
        gather_flat(rows, flat)
        acc[...] = jnp.zeros_like(acc)

    gate = dot(flat[...], gate_w[...])
    upper = dot(flat[...], up_w[...])
    active = (gate * jax.nn.sigmoid(gate) * upper).astype(BF16)
    acc[...] += dot(active, down_w[...])

    @pl.when(step == pl.num_programs(0) - 1)
    def _():
        for i, ref in enumerate(outs):
            ref[...] = acc[i * slots : (i + 1) * slots, :].astype(BF16)


def spread_hot(rank_ref, slots, hot_ref):
    for k in range(rank_ref.shape[0]):
        hot_ref[k * slots : (k + 1) * slots, :] = one_hot(slot_mask(rank_ref, k, slots))


def spread_weights(rank_ref, weight_ref, slots, high_ref, low_ref):
    for k in range(rank_ref.shape[0]):
        rows = slice(k * slots, (k + 1) * slots)
        value = jnp.where(slot_mask(rank_ref, k, slots), weight_ref[k : k + 1, :], 0.0)
        high = value.astype(BF16)
        high_ref[rows, :] = high
        low_ref[rows, :] = (value - high.astype(F32)).astype(BF16)


def grads_far_kernel(half, rank_ref, *refs):
    pieces, (out_ref, table, hot) = refs[:half], refs[half:]
    gather_flat(pieces, table)
    spread_hot(rank_ref, pieces[0].shape[0], hot)
    out_ref[...] = t_dot(hot[...], table[...]).astype(BF16)


def sum_far_kernel(half, rank_ref, weight_ref, *refs):
    pieces, (out_ref, table, high, low) = refs[:half], refs[half:]
    gather_flat(pieces, table)
    spread_weights(rank_ref, weight_ref, pieces[0].shape[0], high, low)
    out_ref[...] = (t_dot(high[...], table[...]) + t_dot(low[...], table[...])).astype(BF16)


def sum_own_kernel(half, rank_ref, weight_ref, x_ref, *refs):
    pieces, (out_ref, table, high, low) = refs[:half], refs[half:]
    gather_flat(pieces, table)
    spread_weights(rank_ref, weight_ref, pieces[0].shape[0], high, low)
    total = t_dot(high[...], table[...]) + t_dot(low[...], table[...])
    out_ref[...] = x_ref[...].astype(F32) + total


def terms_kernel(half, rank_ref, far_rank_ref, *refs):
    inners, (own_ref, far_ref) = refs[:half], refs[half:]
    for b, (rank, out) in enumerate(((rank_ref, own_ref), (far_rank_ref, far_ref))):
        for k in range(half):
            inner = jnp.broadcast_to(inners[k][b : b + 1, :].astype(BF16), (16, inners[k].shape[1]))
            out[k : k + 1, :] = dot(inner, one_hot(slot_mask(rank, k, inner.shape[1])))[:1, :]


def source_kernel(half, top, *refs):
    me_ref, xp_ref, dy_ref, cross_ref, own_ref, gain_ref, router_ref, normed_ref = refs[:8]
    table_ref, lifted_ref, terms_ref, far_terms_ref, grad_ref, sums_ref = refs[8:]
    tokens, experts = xp_ref.shape[0], router_ref.shape[0]
    routes = route_rows(table_ref, 1, top)
    wanted = me_ref[0] ^ iota((half, tokens), 0)
    lifted = [lifted_ref[j : j + 1, :] for j in range(top)]
    dweight = []
    for r in routes:
        near = jnp.where(r == wanted, terms_ref[...], 0.0)
        far = jnp.where(r == (wanted ^ half), far_terms_ref[...], 0.0)
        dweight.append(jnp.sum(near, axis=0, keepdims=True) + jnp.sum(far, axis=0, keepdims=True))
    total = functools.reduce(jnp.add, lifted)
    both = functools.reduce(jnp.add, [d * l for d, l in zip(dweight, lifted)])
    dlogits = jnp.zeros((experts, tokens), F32)
    for r, d, l in zip(routes, dweight, lifted):
        dsel = (d / total - both / (total * total)) * l * (1.0 - l)
        dlogits = dlogits + jnp.where(r == iota((experts, tokens), 0), dsel, 0.0)
    exact = lax.Precision.HIGHEST
    normed = normed_ref[...].astype(F32)
    sums_ref[...] = jnp.zeros_like(sums_ref)
    sums_ref[:experts, :] = jnp.dot(dlogits, normed, precision=exact, preferred_element_type=F32)
    grad_ref_f = own_ref[...] + cross_ref[...].astype(F32)
    dnormed = grad_ref_f + t_dot(dlogits, router_ref[...].astype(F32), precision=exact)
    values = xp_ref[...].astype(F32)
    scale = lax.rsqrt(jnp.mean(values * values, axis=-1, keepdims=True) + EPS)
    bare = values * scale
    sums_ref[experts : experts + 1, :] = jnp.sum(dnormed * bare, axis=0, keepdims=True)
    lifted_grad = dnormed * gain_ref[...]
    slope = jnp.mean(lifted_grad * bare, axis=-1, keepdims=True)
    grad_ref[...] = (dy_ref[...].astype(F32) + scale * (lifted_grad - bare * slope)).astype(BF16)


def grads_own_kernel(half, rank_ref, *refs):
    pieces, (out_ref, table, hot) = refs[:half], refs[half:]
    gather_flat(pieces, table)
    spread_hot(rank_ref, pieces[0].shape[0], hot)
    out_ref[...] = t_dot(hot[...], table[...])


def per_device(
    next_input,
    prev_input,
    next_cot,
    gate_weight,
    up_weight,
    down_weight,
    router,
    gain,
    next_routes,
    prev_routes,
    next_priority,
    prev_priority,
):
    experts = router.shape[-1]
    tokens, width = next_input.shape[1:]
    hidden = gate_weight.shape[-1]
    top = next_routes.shape[-1]
    capacity = (5 * top * tokens + 4 * experts - 1) // (4 * experts)
    slots = -(-capacity // 16) * 16
    gate_w, up_w, down_w = (gate_weight[0, 0], up_weight[0, 0], down_weight[0, 0])
    half = lax.axis_size("expert") // 2
    gain_row, router_t = (gain, router[0].T)
    me = jnp.reshape(lax.axis_index("expert"), (1,)).astype(jnp.int32)
    partial = functools.partial
    smem, vmem = pl.BlockSpec(memory_space=pltpu.SMEM), pl.BlockSpec(memory_space=pltpu.VMEM)
    block = shape((tokens, width))

    table = jnp.concatenate(
        [next_routes[0].T, prev_routes[0].T, next_priority, prev_priority], axis=0
    )
    far_table = hop(table, 0, half, "tables")
    xp_own = prev_input[0]
    xp_far = hop(xp_own, 0, half, "xp_far")
    dy_own = hop(next_cot[0], -1, 0, "dy_own")
    x_own = hop(next_input[0], 1, 0, "x_own")
    dy_far = hop(after(next_cot[0], xp_far), -1, half, "dy_far")
    x_far = hop(after(next_input[0], dy_far), 1, half, "x_far")

    frank_own, rank_own, frank_far, rank_far = call(
        partial(rank_kernel, capacity, half, top),
        "ranks",
        [shape((half, tokens), jnp.int32)] * 4,
        [me, table, far_table],
        in_specs=[smem, vmem, vmem],
    )

    weights_shape = shape((half, tokens), F32)
    scales_shape = shape((half, slots), F32)
    outs = call(
        partial(own_kernel, half, top),
        "own_rows",
        [shape((3, slots, width))] * half
        + [block, shape((top, tokens), F32), weights_shape, scales_shape, weights_shape],
        [me, xp_own, dy_own, x_own, gain_row, router_t, table, frank_own, rank_own],
        in_specs=[smem] + [vmem] * 8,
        scratch=[pltpu.VMEM((tokens, width), BF16)],
    )
    own = exchange(outs[:half], "own_rows")
    normed, lifted, _, scale_own, fweight_own = outs[half:]

    def far_rows(x, batch, rank, name):
        outs = call(
            partial(far_kernel, half, top, batch),
            name,
            [shape((slots, width))] * half + [weights_shape, scales_shape],
            [me, x, gain_row, router_t, far_table, rank],
            in_specs=[smem] + [vmem] * 5,
            scratch=[pltpu.VMEM((tokens, width), BF16)],
        )
        return exchange(outs[:half], name), outs[half], outs[half + 1]

    rows_far, _, scale_far = far_rows(xp_far, 1, rank_far, "rows_far")
    scales = exchange([jnp.stack([scale_own[k], scale_far[k]]) for k in range(half)], "scales")
    cot_far = call(plain_kernel, "cot_far", [shape((slots, width))] * half, [rank_far, dy_far])
    cot_far = exchange(cot_far, "cot_far")
    frows_far, fweight_far, _ = far_rows(x_far, 0, frank_far, "frows_far")

    part = 256 if hidden % 256 == 0 else hidden
    grid = (hidden // part,)
    across = pl.BlockSpec((width, part), lambda f: (0, f))
    down_spec = pl.BlockSpec((part, width), lambda f: (f, 0))
    mats, mat_specs = [gate_w, up_w, down_w], [across, across, down_spec]
    piece = pl.BlockSpec((slots, width), lambda f: (0, 0))
    rows = 2 * half * slots
    flops = 2 * rows * width * hidden

    def of_own(which):
        return pl.BlockSpec((1, slots, width), lambda f: (which, 0, 0))

    def whole(*dims):
        return pl.BlockSpec(dims, lambda f: (0,) * len(dims))

    hidden_spec = pl.BlockSpec((rows, part), lambda f: (0, f))
    flat, gate, upper, active, result = call(
        partial(hidden_kernel, 2 * half),
        "hidden",
        [shape((rows, width))]
        + [shape((rows, hidden), F32)] * 2
        + [shape((rows, hidden)), shape((rows, width))],
        own + rows_far + mats,
        grid=grid,
        in_specs=[of_own(0)] * half + [piece] * half + mat_specs,
        out_specs=[whole(rows, width)] + [hidden_spec] * 3 + [whole(rows, width)],
        scratch=[pltpu.VMEM((rows, width), F32)],
        flops=3 * flops,
    )
    outs = call(
        partial(back_kernel, 2 * half, half),
        "back",
        [shape((slots, width))] * (2 * half)
        + [shape((2, slots), F32)] * half
        + [shape((rows, width)), shape((rows, hidden)), shape((rows, hidden))],
        own + cot_far + scales + mats + [gate, upper, result],
        grid=grid,
        in_specs=[of_own(1)] * half
        + [piece] * half
        + [whole(2, slots)] * half
        + mat_specs
        + [hidden_spec] * 2
        + [whole(rows, width)],
        out_specs=[piece] * (2 * half)
        + [whole(2, slots)] * half
        + [whole(rows, width)]
        + [hidden_spec] * 2,
        scratch=[pltpu.VMEM((rows, width), F32)],
        flops=3 * flops,
    )
    grads, inner = outs[: 2 * half], outs[2 * half : 3 * half]
    scaled, gate_part, up_part = outs[3 * half :]
    grads_far = exchange(grads[half:], "grads_far")
    grads_own = exchange(grads[:half], "grads_own")
    inner = exchange(inner, "inner")
    gate_wgrad = t_dot(flat, gate_part).astype(BF16)
    up_wgrad = t_dot(flat, up_part).astype(BF16)
    down_wgrad = t_dot(active, scaled).astype(BF16)

    def forward_part(pieces, specs, name):
        outs = call(
            partial(forward_kernel, half),
            name,
            [shape((slots, width))] * half,
            pieces + mats,
            grid=grid,
            in_specs=specs + mat_specs,
            out_specs=[piece] * half,
            scratch=[
                pltpu.VMEM((half * slots, width), BF16),
                pltpu.VMEM((half * slots, width), F32),
            ],
            flops=3 * flops // 2,
        )
        return exchange(outs, name)

    out_own = forward_part(own, [of_own(2)] * half, "out_own")
    out_far = forward_part(frows_far, [piece] * half, "out_far")

    table_scratch = pltpu.VMEM((half * slots, width), BF16)
    hot_scratch = pltpu.VMEM((half * slots, tokens), BF16)
    (grads_sum,) = call(
        partial(grads_far_kernel, half),
        "grads_sum",
        [block],
        [rank_far] + grads_far,
        scratch=[table_scratch, hot_scratch],
    )
    grads_cross = hop(grads_sum, 0, half, "grads_cross")
    terms, far_terms = call(
        partial(terms_kernel, half), "terms", [weights_shape] * 2, [rank_own, rank_far] + inner
    )
    far_terms = hop(far_terms, 0, half, "terms")
    (out_sum,) = call(
        partial(sum_far_kernel, half),
        "out_sum",
        [block],
        [frank_far, fweight_far] + out_far,
        scratch=[table_scratch, hot_scratch, hot_scratch],
    )
    out_cross = hop(after(out_sum, grads_cross), 0, half, "out_cross")
    (grads_near,) = call(
        partial(grads_own_kernel, half),
        "grads_near",
        [shape((tokens, width), F32)],
        [rank_own] + grads_own,
        scratch=[table_scratch, hot_scratch],
    )
    (out_near,) = call(
        partial(sum_own_kernel, half),
        "out_near",
        [shape((tokens, width), F32)],
        [frank_own, fweight_own, x_own] + out_own,
        scratch=[table_scratch, hot_scratch, hot_scratch],
    )

    sum_rows = -(-(experts + 1) // 8) * 8
    grad_in, sums = call(
        partial(source_kernel, half, top),
        "source",
        [block, shape((sum_rows, width), F32)],
        [me, xp_own, dy_own, grads_cross, grads_near, gain_row, router_t, normed]
        + [table, lifted, terms, far_terms],
        in_specs=[smem] + [vmem] * 11,
    )
    step = 1
    while step < lax.axis_size("expert"):
        sums = sums + hop(sums, 0, step, "sums")
        step *= 2
    forward = (out_near + out_cross.astype(F32)).astype(BF16)
    return (
        forward[None],
        grad_in[None],
        gate_wgrad[None, None],
        up_wgrad[None, None],
        down_wgrad[None, None],
        sums[:experts].T[None],
        sums[experts][None],
    )


def solution(mesh):
    rows = P("pipe", "expert", None)
    weights = P("pipe", "expert", None, None)
    shared = P("pipe", None, None)
    return jax.shard_map(
        per_device,
        mesh=mesh,
        in_specs=(rows,) * 3
        + (weights,) * 3
        + (shared, P("pipe", None), rows, rows, P("pipe", "expert"), P("pipe", "expert")),
        out_specs=(rows, rows, weights, weights, weights, shared, P("pipe", None)),
        check_vma=False,
    )
```

```python
import functools

import jax
import jax.numpy as jnp
from jax import lax
from jax.experimental import pallas as pl
from jax.experimental.pallas import tpu as pltpu
from jax.sharding import PartitionSpec as P

EPS = 1e-06
F32 = jnp.float32
BF16 = jnp.bfloat16
VMEM_BYTES = 56 * 1024 * 1024
LANES = 128
SCALE = 64


def hop(block, pipe_step, flip, name):
    pipes, experts = lax.axis_size("pipe"), lax.axis_size("expert")
    with jax.named_scope(name):
        if pipe_step == 0:
            return lax.ppermute(block, "expert", [(e, e ^ flip) for e in range(experts)])
        route = [
            (p * experts + e, ((p + pipe_step) % pipes) * experts + (e ^ flip))
            for p in range(pipes)
            for e in range(experts)
        ]
        return lax.ppermute(block, ("pipe", "expert"), route)


def after(block, *earlier):
    return lax.optimization_barrier((block,) + earlier)[0]


def dot(a, b):
    return jnp.dot(a, b, preferred_element_type=F32)


def dot_t(a, b):
    return lax.dot_general(a, b, (((1,), (1,)), ((), ())), preferred_element_type=F32)


def t_dot(a, b, precision=None):
    dims = (((0,), (0,)), ((), ()))
    return lax.dot_general(a, b, dims, preferred_element_type=F32, precision=precision)


def iota(shape, dim):
    return lax.broadcasted_iota(jnp.int32, shape, dim)


def call(kernel, name, outs, ins, grid=(), in_specs=None, out_specs=None, scratch=(), flops=0):
    whole = pl.BlockSpec(memory_space=pltpu.VMEM)
    moved = sum(a.size * a.dtype.itemsize for a in list(outs) + list(ins))
    return pl.pallas_call(
        kernel,
        out_shape=[jax.ShapeDtypeStruct(o.shape, o.dtype) for o in outs],
        grid=grid,
        in_specs=in_specs or [whole] * len(ins),
        out_specs=out_specs or [whole] * len(outs),
        scratch_shapes=list(scratch),
        compiler_params=pltpu.CompilerParams(vmem_limit_bytes=VMEM_BYTES),
        cost_estimate=pl.CostEstimate(flops=flops // SCALE, bytes_accessed=moved // SCALE, transcendentals=0),
        name=name,
    )(*ins)


def shape(dims, dtype=BF16):
    return jax.ShapeDtypeStruct(tuple(dims), dtype)


def rank_kernel(capacity, top, table_ref, *rank_refs):
    experts, tokens = rank_refs[0].shape
    for batch, rank_ref in enumerate(rank_refs):
        row = 2 * top + batch
        order = jnp.broadcast_to(table_ref[row : row + 1, :], (tokens, tokens))
        before = (order.T < order).astype(F32).astype(BF16)
        chosen = iota((experts, tokens), 0) < 0
        for routes in route_rows(table_ref, batch, top):
            chosen = chosen | (routes == iota((experts, tokens), 0))
        count = dot(chosen.astype(F32).astype(BF16), before)
        rank_ref[...] = jnp.where(chosen & (count < capacity), count.astype(jnp.int32), -1)


def route_rows(ref, batch, top):
    return [ref[batch * top + j : batch * top + j + 1, :] for j in range(top)]


def slot_mask(rank_ref, e, slots):
    rank = rank_ref[e : e + 1, :]
    return iota((slots, rank.shape[1]), 0) == rank


def one_hot(mask):
    return jnp.where(mask, 1.0, 0.0).astype(BF16)


def normalise(x_ref, gain_ref, normed_ref, step=32):
    def part(i, carry):
        rows = pl.ds(pl.multiple_of(i * step, step), step)
        values = x_ref[rows, :].astype(F32)
        scale = lax.rsqrt(jnp.mean(values * values, axis=-1, keepdims=True) + EPS)
        normed_ref[rows, :] = (values * scale * gain_ref[...]).astype(BF16)
        return carry

    lax.fori_loop(0, x_ref.shape[0] // step, part, 0)


def gates(normed_ref, router_ref, routes, lifted_ref, weight_ref):
    logits = dot_t(router_ref[...], normed_ref[...])
    everyone = iota(logits.shape, 0)
    lifted = [
        jax.nn.sigmoid(jnp.sum(jnp.where(r == everyone, logits, 0.0), axis=0, keepdims=True))
        for r in routes
    ]
    total = functools.reduce(jnp.add, lifted)
    weight = jnp.zeros(weight_ref.shape, F32)
    for j, (r, value) in enumerate(zip(routes, lifted)):
        if lifted_ref is not None:
            lifted_ref[j : j + 1, :] = value
        weight = weight + jnp.where(r == everyone, value / total, 0.0)
    weight_ref[...] = weight


def put_rows(rank_ref, block_ref, message_ref):
    for e in range(message_ref.shape[0]):
        hot = one_hot(slot_mask(rank_ref, e, message_ref.shape[1]))
        message_ref[e] = dot(hot, block_ref[...]).astype(BF16)


def rows_kernel(batch, top, *refs):
    x_ref, gain_ref, router_ref, table_ref, rank_ref = refs[:5]
    message_ref, weight_ref, normed_ref, lifted_ref = (*refs[5:], None)[:4]
    normalise(x_ref, gain_ref, normed_ref)
    put_rows(rank_ref, normed_ref, message_ref)
    gates(normed_ref, router_ref, route_rows(table_ref, batch, top), lifted_ref, weight_ref)


def cots_kernel(rank_ref, weight_ref, x_ref, message_ref):
    width = x_ref.shape[1]
    for e in range(message_ref.shape[0]):
        hot = one_hot(slot_mask(rank_ref, e, message_ref.shape[1]))
        message_ref[e, :, :width] = dot(hot, x_ref[...]).astype(BF16)
        weight = weight_ref[e : e + 1, :].astype(BF16)
        weight = jnp.broadcast_to(weight, (LANES, weight.shape[1]))
        message_ref[e, :, width:] = dot_t(hot, weight).astype(BF16)


def flat_of(ref):
    return ref[...].reshape(-1, ref.shape[-1])


def add(acc, value):
    step = pl.program_id(0)

    @pl.when(step == 0)
    def _():
        acc[...] = value

    @pl.when(step > 0)
    def _():
        acc[...] += value


def expert_kernel(rows_ref, cot_ref, gate_w, up_w, down_w, *refs):
    message_ref, scaled_ref, active_ref, gate_part_ref, up_part_ref, acc_out, acc_grad = refs
    senders, slots, width = rows_ref.shape

    @pl.when(pl.program_id(0) == 0)
    def _():
        for k in range(senders):
            scale = cot_ref[k, :, width:].astype(F32)[:, :1]
            scaled = (scale * cot_ref[k, :, :width].astype(F32)).astype(BF16)
            scaled_ref[k * slots : (k + 1) * slots, :] = scaled

    rows = flat_of(rows_ref)
    gate = dot(rows, gate_w[...])
    upper = dot(rows, up_w[...])
    sig = jax.nn.sigmoid(gate)
    active = (gate * sig * upper).astype(BF16)
    active_ref[...] = active
    act_grad = dot_t(scaled_ref[...], down_w[...])
    gate_part = (act_grad * upper * sig * (1.0 + gate * (1.0 - sig))).astype(BF16)
    up_part = (act_grad * (gate * sig)).astype(BF16)
    gate_part_ref[...] = gate_part
    up_part_ref[...] = up_part
    add(acc_grad, dot_t(gate_part, gate_w[...]) + dot_t(up_part, up_w[...]))
    add(acc_out, dot(active, down_w[...]))

    @pl.when(pl.program_id(0) == pl.num_programs(0) - 1)
    def _():
        for k in range(senders):
            part = slice(k * slots, (k + 1) * slots)
            message_ref[k, :, :width] = acc_grad[part, :].astype(BF16)
            result = acc_out[part, :].astype(BF16).astype(F32)
            cot = cot_ref[k, :, :width].astype(F32)
            inner = jnp.sum(cot * result, axis=1, keepdims=True).astype(BF16)
            message_ref[k, :, width:] = jnp.broadcast_to(inner, (slots, LANES))


def forward_kernel(rows_ref, gate_w, up_w, down_w, out_ref, acc):
    rows = flat_of(rows_ref)
    gate = dot(rows, gate_w[...])
    active = (gate * jax.nn.sigmoid(gate) * dot(rows, up_w[...])).astype(BF16)
    add(acc, dot(active, down_w[...]))

    @pl.when(pl.program_id(0) == pl.num_programs(0) - 1)
    def _():
        out_ref[...] = acc[...].astype(BF16).reshape(out_ref.shape)


def out_kernel(rank_ref, weight_ref, x_ref, rows_ref, out_ref, high_ref, low_ref):
    slots = rows_ref.shape[1]
    for e in range(rank_ref.shape[0]):
        part = slice(e * slots, (e + 1) * slots)
        value = jnp.where(slot_mask(rank_ref, e, slots), weight_ref[e : e + 1, :], 0.0)
        high = value.astype(BF16)
        high_ref[part, :] = high
        low_ref[part, :] = (value - high.astype(F32)).astype(BF16)
    rows = flat_of(rows_ref)
    total = t_dot(high_ref[...], rows) + t_dot(low_ref[...], rows)
    out_ref[...] = (x_ref[...].astype(F32) + total).astype(BF16)


def source_kernel(top, *refs):
    rank_ref, grads_ref, table_ref, lifted_ref = refs[:4]
    router_ref, normed_ref, xp_ref, dy_ref, gain_ref = refs[4:9]
    grad_ref, sums_ref, hot_ref, terms_ref = refs[9:]
    experts, tokens = rank_ref.shape
    slots, width = grads_ref.shape[1], xp_ref.shape[1]
    for e in range(experts):
        hot = one_hot(slot_mask(rank_ref, e, slots))
        hot_ref[e * slots : (e + 1) * slots, :] = hot
        terms_ref[e : e + 1, :] = t_dot(grads_ref[e, :, width:], hot)[:1, :]
    routes = route_rows(table_ref, 1, top)
    everyone = iota((experts, tokens), 0)
    lifted = [lifted_ref[j : j + 1, :] for j in range(top)]
    dweight = [
        jnp.sum(jnp.where(r == everyone, terms_ref[...], 0.0), axis=0, keepdims=True)
        for r in routes
    ]
    total = functools.reduce(jnp.add, lifted)
    both = functools.reduce(jnp.add, [d * l for d, l in zip(dweight, lifted)])
    dlogits = jnp.zeros((experts, tokens), F32)
    for r, d, l in zip(routes, dweight, lifted):
        dsel = (d / total - both / (total * total)) * l * (1.0 - l)
        dlogits = dlogits + jnp.where(r == everyone, dsel, 0.0)
    exact = lax.Precision.HIGHEST
    normed = normed_ref[...].astype(F32)
    sums_ref[...] = jnp.zeros_like(sums_ref)
    sums_ref[:experts, :] = jnp.dot(dlogits, normed, precision=exact, preferred_element_type=F32)
    dnormed = t_dot(hot_ref[...], grads_ref[:, :, :width].reshape(-1, width))
    dnormed = dnormed + t_dot(dlogits, router_ref[...].astype(F32), precision=exact)
    values = xp_ref[...].astype(F32)
    scale = lax.rsqrt(jnp.mean(values * values, axis=-1, keepdims=True) + EPS)
    bare = values * scale
    sums_ref[experts : experts + 1, :] = jnp.sum(dnormed * bare, axis=0, keepdims=True)
    lifted_grad = dnormed * gain_ref[...]
    slope = jnp.mean(lifted_grad * bare, axis=-1, keepdims=True)
    grad_ref[...] = (dy_ref[...].astype(F32) + scale * (lifted_grad - bare * slope)).astype(BF16)


def per_device(
    next_input,
    prev_input,
    next_cot,
    gate_weight,
    up_weight,
    down_weight,
    router,
    gain,
    next_routes,
    prev_routes,
    next_priority,
    prev_priority,
):
    experts = router.shape[-1]
    tokens, width = next_input.shape[1:]
    hidden = gate_weight.shape[-1]
    top = next_routes.shape[-1]
    capacity = (5 * top * tokens + 4 * experts - 1) // (4 * experts)
    slots = -(-capacity // 16) * 16
    mats = [gate_weight[0, 0], up_weight[0, 0], down_weight[0, 0]]
    gain_row, router_t = (gain, router[0].T)
    partial = functools.partial
    block, message = shape((tokens, width)), shape((experts, slots, width))
    per_token, longer = shape((experts, tokens), F32), shape((experts, slots, width + LANES))

    def exchange(array, name):
        with jax.named_scope(name):
            return lax.all_to_all(array, "expert", 0, 0, tiled=True)

    dy_in = hop(next_cot[0], -1, 0, "dy_in")
    x_in = hop(next_input[0], 1, 0, "x_in")
    xp = prev_input[0]
    table = jnp.concatenate(
        [next_routes[0].T, prev_routes[0].T, next_priority, prev_priority], axis=0
    )
    frank, rank = call(
        partial(rank_kernel, capacity, top), "ranks", [shape((experts, tokens), jnp.int32)] * 2, [table]
    )
    rows, weight, normed, lifted = call(
        partial(rows_kernel, 1, top),
        "rows",
        [message, per_token, block, shape((top, tokens), F32)],
        [xp, gain_row, router_t, table, rank],
    )
    rows = exchange(rows, "rows")
    (cots,) = call(cots_kernel, "cots", [longer], [rank, weight, dy_in])
    cots = exchange(after(cots, rows), "cots")
    frows, fweight = call(
        partial(rows_kernel, 0, top),
        "frows",
        [message, per_token],
        [x_in, gain_row, router_t, table, frank],
        scratch=[pltpu.VMEM((tokens, width), BF16)],
    )
    frows = exchange(after(frows, cots), "frows")

    part = 256 if hidden % 256 == 0 else hidden
    grid = (hidden // part,)
    across = pl.BlockSpec((width, part), lambda f: (0, f))
    mat_specs = [across, across, pl.BlockSpec((part, width), lambda f: (f, 0))]
    count = experts * slots
    flops = 2 * count * width * hidden

    def whole(array):
        dims = array.shape
        return pl.BlockSpec(dims, lambda f: (0,) * len(dims), pipeline_mode=pl.Buffered(1))

    hidden_spec = pl.BlockSpec((count, part), lambda f: (0, f))
    wide = pltpu.VMEM((count, width), F32)
    flat = shape((count, width))
    grads, scaled, active, gate_part, up_part = call(
        expert_kernel,
        "expert",
        [longer, flat] + [shape((count, hidden))] * 3,
        [rows, cots] + mats,
        grid=grid,
        in_specs=[whole(message), whole(longer)] + mat_specs,
        out_specs=[whole(longer), whole(flat)] + [hidden_spec] * 3,
        scratch=[wide] * 2,
        flops=6 * flops,
    )
    grads = exchange(after(grads, frows), "grads")
    (outs,) = call(
        forward_kernel,
        "forward",
        [message],
        [frows] + mats,
        grid=grid,
        in_specs=[whole(message)] + mat_specs,
        out_specs=[whole(message)],
        scratch=[wide],
        flops=3 * flops,
    )
    outs = exchange(after(outs, grads), "outs")
    flat_rows = rows.reshape(count, width)
    gate_wgrad = t_dot(flat_rows, gate_part).astype(BF16)
    up_wgrad = t_dot(flat_rows, up_part).astype(BF16)
    down_wgrad = t_dot(active, scaled).astype(BF16)

    grad_in, sums = call(
        partial(source_kernel, top),
        "source",
        [block, shape((-(-(experts + 1) // 8) * 8, width), F32)],
        [rank, grads, table, lifted, router_t, normed, xp, dy_in, gain_row],
        scratch=[pltpu.VMEM((count, tokens), BF16), pltpu.VMEM((experts, tokens), F32)],
    )
    step = 1
    while step < lax.axis_size("expert"):
        sums = sums + hop(sums, 0, step, "sums")
        step *= 2
    (forward,) = call(
        out_kernel,
        "out",
        [block],
        [frank, fweight, x_in, outs],
        scratch=[pltpu.VMEM((count, tokens), BF16)] * 2,
    )
    return (
        forward[None],
        grad_in[None],
        gate_wgrad[None, None],
        up_wgrad[None, None],
        down_wgrad[None, None],
        sums[:experts].T[None],
        sums[experts][None],
    )


def solution(mesh):
    rows = P("pipe", "expert", None)
    weights = P("pipe", "expert", None, None)
    shared = P("pipe", None, None)
    return jax.shard_map(
        per_device,
        mesh=mesh,
        in_specs=(rows,) * 3
        + (weights,) * 3
        + (shared, P("pipe", None), rows, rows, P("pipe", "expert"), P("pipe", "expert")),
        out_specs=(rows, rows, weights, weights, weights, shared, P("pipe", None)),
        check_vma=False,
    )
```

```python
import functools

import jax
import jax.numpy as jnp
from jax import lax
from jax.experimental import pallas as pl
from jax.experimental.pallas import tpu as pltpu
from jax.sharding import PartitionSpec as P

EPS = 1e-06
F32 = jnp.float32
BF16 = jnp.bfloat16
VMEM_BYTES = 56 * 1024 * 1024
LANES = 128
SCALE = 64


def hop(block, pipe_step, flip, name):
    pipes, experts = lax.axis_size("pipe"), lax.axis_size("expert")
    with jax.named_scope(name):
        if pipe_step == 0:
            return lax.ppermute(block, "expert", [(e, e ^ flip) for e in range(experts)])
        route = [
            (p * experts + e, ((p + pipe_step) % pipes) * experts + (e ^ flip))
            for p in range(pipes)
            for e in range(experts)
        ]
        return lax.ppermute(block, ("pipe", "expert"), route)


def after(block, *earlier):
    return lax.optimization_barrier((block,) + earlier)[0]


def dot(a, b):
    return jnp.dot(a, b, preferred_element_type=F32)


def dot_t(a, b):
    return lax.dot_general(a, b, (((1,), (1,)), ((), ())), preferred_element_type=F32)


def t_dot(a, b, precision=None):
    dims = (((0,), (0,)), ((), ()))
    return lax.dot_general(a, b, dims, preferred_element_type=F32, precision=precision)


def iota(shape, dim):
    return lax.broadcasted_iota(jnp.int32, shape, dim)


def call(kernel, name, outs, ins, grid=(), in_specs=None, out_specs=None, scratch=(), flops=0):
    whole = pl.BlockSpec(memory_space=pltpu.VMEM)
    moved = sum(a.size * a.dtype.itemsize for a in list(outs) + list(ins))
    return pl.pallas_call(
        kernel,
        out_shape=[jax.ShapeDtypeStruct(o.shape, o.dtype) for o in outs],
        grid=grid,
        in_specs=in_specs or [whole] * len(ins),
        out_specs=out_specs or [whole] * len(outs),
        scratch_shapes=list(scratch),
        compiler_params=pltpu.CompilerParams(vmem_limit_bytes=VMEM_BYTES),
        cost_estimate=pl.CostEstimate(flops=flops // SCALE, bytes_accessed=moved // SCALE, transcendentals=0),
        name=name,
    )(*ins)


def shape(dims, dtype=BF16):
    return jax.ShapeDtypeStruct(tuple(dims), dtype)


def rank_kernel(capacity, top, table_ref, *rank_refs):
    experts, tokens = rank_refs[0].shape
    for batch, rank_ref in enumerate(rank_refs):
        row = 2 * top + batch
        order = jnp.broadcast_to(table_ref[row : row + 1, :], (tokens, tokens))
        before = (order.T < order).astype(F32).astype(BF16)
        chosen = iota((experts, tokens), 0) < 0
        for routes in route_rows(table_ref, batch, top):
            chosen = chosen | (routes == iota((experts, tokens), 0))
        count = dot(chosen.astype(F32).astype(BF16), before)
        rank_ref[...] = jnp.where(chosen & (count < capacity), count.astype(jnp.int32), -1)


def route_rows(ref, batch, top):
    return [ref[batch * top + j : batch * top + j + 1, :] for j in range(top)]


def slot_mask(rank_ref, e, slots):
    rank = rank_ref[e : e + 1, :]
    return iota((slots, rank.shape[1]), 0) == rank


def one_hot(mask):
    return jnp.where(mask, 1.0, 0.0).astype(BF16)


def normalise(x_ref, gain_ref, normed_ref, step=32):
    def part(i, carry):
        rows = pl.ds(pl.multiple_of(i * step, step), step)
        values = x_ref[rows, :].astype(F32)
        scale = lax.rsqrt(jnp.mean(values * values, axis=-1, keepdims=True) + EPS)
        normed_ref[rows, :] = (values * scale * gain_ref[...]).astype(BF16)
        return carry

    lax.fori_loop(0, x_ref.shape[0] // step, part, 0)


def gates(normed_ref, router_ref, routes, lifted_ref, weight_ref):
    logits = dot_t(router_ref[...], normed_ref[...])
    everyone = iota(logits.shape, 0)
    lifted = [
        jax.nn.sigmoid(jnp.sum(jnp.where(r == everyone, logits, 0.0), axis=0, keepdims=True))
        for r in routes
    ]
    total = functools.reduce(jnp.add, lifted)
    weight = jnp.zeros(weight_ref.shape, F32)
    for j, (r, value) in enumerate(zip(routes, lifted)):
        if lifted_ref is not None:
            lifted_ref[j : j + 1, :] = value
        weight = weight + jnp.where(r == everyone, value / total, 0.0)
    weight_ref[...] = weight


def put_pieces(me_ref, rank_ref, block_ref, weight_ref, pieces):
    width = block_ref.shape[1]
    for k, piece in enumerate(pieces):
        expert = pl.ds(me_ref[0] ^ k, 1)
        rank = rank_ref[expert, :]
        hot = one_hot(iota((piece.shape[0], rank.shape[1]), 0) == rank)
        piece[:, :width] = dot(hot, block_ref[...]).astype(BF16)
        if weight_ref is not None:
            weight = weight_ref[expert, :].astype(BF16)
            weight = jnp.broadcast_to(weight, (LANES, weight.shape[1]))
            piece[:, width:] = dot_t(hot, weight).astype(BF16)


def own_kernel(half, batch, top, *refs):
    me_ref, x_ref, gain_ref, router_ref, table_ref, rank_ref = refs[:6]
    pieces, (weight_ref, normed_ref, lifted_ref) = refs[6 : 6 + half], (*refs[6 + half :], None)[:3]
    normalise(x_ref, gain_ref, normed_ref)
    gates(normed_ref, router_ref, route_rows(table_ref, batch, top), lifted_ref, weight_ref)
    put_pieces(me_ref, rank_ref, normed_ref, weight_ref if batch else None, pieces)


def far_kernel(half, batch, top, *refs):
    me_ref, x_ref, gain_ref, router_ref, table_ref, rank_ref = refs[:6]
    pieces, (normed_ref, weight_ref) = refs[6 : 6 + half], refs[6 + half :]
    normalise(x_ref, gain_ref, normed_ref)
    if batch:
        gates(normed_ref, router_ref, route_rows(table_ref, batch, top), None, weight_ref)
    put_pieces(me_ref, rank_ref, normed_ref, weight_ref if batch else None, pieces)


def rows_kernel(top, *refs):
    x_ref, gain_ref, router_ref, table_ref, rank_ref, message_ref, weight_ref, normed_ref = refs
    normalise(x_ref, gain_ref, normed_ref)
    cots_kernel(rank_ref, normed_ref, message_ref)
    gates(normed_ref, router_ref, route_rows(table_ref, 0, top), None, weight_ref)


def cots_kernel(rank_ref, x_ref, message_ref):
    for e in range(message_ref.shape[0]):
        hot = one_hot(slot_mask(rank_ref, e, message_ref.shape[1]))
        message_ref[e] = dot(hot, x_ref[...]).astype(BF16)


def flat_of(ref):
    return ref[...].reshape(-1, ref.shape[-1])


def each_sender(me_ref, count, slots):
    for k in range(count):
        sender = me_ref[0] ^ k
        yield k, sender, pl.ds(pl.multiple_of(sender * slots, 16), slots)


def expert_kernel(steps, half, *refs):
    me_ref, gate_a, up_a, down_a, gate_b, up_b, down_b, cot_ref = refs[:8]
    pieces, refs = refs[8 : 8 + 2 * half], refs[8 + 2 * half :]
    message_ref, rows_ref, scaled_ref, active_ref, gate_part_ref, up_part_ref, inner_ref = refs
    slots = pieces[0].shape[0]
    width = rows_ref.shape[1]
    step = pl.program_id(0)

    @pl.when(step == 0)
    def _():
        for k, sender, part in each_sender(me_ref, 2 * half, slots):
            rows_ref[part, :] = pieces[k][:, :width]
            scale = pieces[k][:, width:].astype(F32)[:, :1]
            scaled_ref[part, :] = (scale * cot_ref[sender].astype(F32)).astype(BF16)
        inner_ref[...] = jnp.zeros_like(inner_ref)

    @pl.when(step < steps)
    def _():
        gate = dot(rows_ref[...], gate_a[...])
        upper = dot(rows_ref[...], up_a[...])
        sig = jax.nn.sigmoid(gate)
        act_grad = dot_t(scaled_ref[...], down_a[...])
        active_ref[step] = (gate * sig * upper).astype(BF16)
        gate_part_ref[step] = (act_grad * upper * sig * (1.0 + gate * (1.0 - sig))).astype(BF16)
        up_part_ref[step] = (act_grad * (gate * sig)).astype(BF16)

    @pl.when(step >= steps)
    def _():
        part = gate_a.shape[1]
        columns = pl.ds(pl.multiple_of((step - steps) * gate_b.shape[0], 128), gate_b.shape[0])
        total = jnp.zeros((rows_ref.shape[0], gate_b.shape[0]), F32)
        result = total
        for f in range(steps):
            hidden = slice(f * part, (f + 1) * part)
            total = total + dot_t(gate_part_ref[f], gate_b[:, hidden])
            total = total + dot_t(up_part_ref[f], up_b[:, hidden])
            result = result + dot(active_ref[f], down_b[hidden, :])
        message_ref[:, columns] = total.astype(BF16)
        cot = cot_ref[:, :, columns].reshape(total.shape).astype(F32)
        result = result.astype(BF16).astype(F32)
        inner_ref[...] += jnp.sum(cot * result, axis=1, keepdims=True)

    @pl.when(step == pl.num_programs(0) - 1)
    def _():
        inner = inner_ref[...].astype(BF16)
        message_ref[:, width:] = jnp.broadcast_to(inner, (inner.shape[0], LANES))


def forward_kernel(steps, rows_ref, gate_a, up_a, down_b, out_ref, active_ref):
    step = pl.program_id(0)

    @pl.when(step < steps)
    def _():
        rows = flat_of(rows_ref)
        gate = dot(rows, gate_a[...])
        active_ref[step] = (gate * jax.nn.sigmoid(gate) * dot(rows, up_a[...])).astype(BF16)

    @pl.when(step >= steps)
    def _():
        part = gate_a.shape[1]
        result = jnp.zeros(active_ref.shape[1:2] + down_b.shape[1:], F32)
        for f in range(steps):
            result = result + dot(active_ref[f], down_b[f * part : (f + 1) * part, :])
        out_ref[...] = result.astype(BF16).reshape(out_ref.shape)


def spread_kernel(slots, rank_ref, weight_ref, spread_ref, flat_ref):
    for e in range(rank_ref.shape[0]):
        mask = slot_mask(rank_ref, e, slots)
        flat_ref[e * slots : (e + 1) * slots, :] = jnp.where(mask, weight_ref[e : e + 1, :], 0.0)
    spread_ref[...] = flat_ref[...].T.astype(BF16)


def source_kernel(top, *refs):
    rank_ref, grads_ref, table_ref, lifted_ref = refs[:4]
    router_ref, normed_ref, xp_ref, dy_ref, gain_ref = refs[4:9]
    grad_ref, sums_ref, hot_ref, terms_ref = refs[9:]
    experts, tokens = rank_ref.shape
    slots, width = grads_ref.shape[1], xp_ref.shape[1]
    for e in range(experts):
        hot = one_hot(slot_mask(rank_ref, e, slots))
        hot_ref[e * slots : (e + 1) * slots, :] = hot
        terms_ref[e : e + 1, :] = t_dot(grads_ref[e, :, width:], hot)[:1, :]
    routes = route_rows(table_ref, 1, top)
    everyone = iota((experts, tokens), 0)
    lifted = [lifted_ref[j : j + 1, :] for j in range(top)]
    dweight = [
        jnp.sum(jnp.where(r == everyone, terms_ref[...], 0.0), axis=0, keepdims=True)
        for r in routes
    ]
    total = functools.reduce(jnp.add, lifted)
    both = functools.reduce(jnp.add, [d * l for d, l in zip(dweight, lifted)])
    dlogits = jnp.zeros((experts, tokens), F32)
    for r, d, l in zip(routes, dweight, lifted):
        dsel = (d / total - both / (total * total)) * l * (1.0 - l)
        dlogits = dlogits + jnp.where(r == everyone, dsel, 0.0)
    exact = lax.Precision.HIGHEST
    normed = normed_ref[...].astype(F32)
    sums_ref[...] = jnp.zeros_like(sums_ref)
    sums_ref[:experts, :] = jnp.dot(dlogits, normed, precision=exact, preferred_element_type=F32)
    dnormed = t_dot(hot_ref[...], grads_ref[:, :, :width].reshape(-1, width))
    dnormed = dnormed + t_dot(dlogits, router_ref[...].astype(F32), precision=exact)
    values = xp_ref[...].astype(F32)
    scale = lax.rsqrt(jnp.mean(values * values, axis=-1, keepdims=True) + EPS)
    bare = values * scale
    sums_ref[experts : experts + 1, :] = jnp.sum(dnormed * bare, axis=0, keepdims=True)
    lifted_grad = dnormed * gain_ref[...]
    slope = jnp.mean(lifted_grad * bare, axis=-1, keepdims=True)
    grad_ref[...] = (dy_ref[...].astype(F32) + scale * (lifted_grad - bare * slope)).astype(BF16)


def per_device(
    next_input,
    prev_input,
    next_cot,
    gate_weight,
    up_weight,
    down_weight,
    router,
    gain,
    next_routes,
    prev_routes,
    next_priority,
    prev_priority,
):
    experts = router.shape[-1]
    tokens, width = next_input.shape[1:]
    hidden = gate_weight.shape[-1]
    top = next_routes.shape[-1]
    capacity = (5 * top * tokens + 4 * experts - 1) // (4 * experts)
    slots = -(-capacity // 16) * 16
    mats = [gate_weight[0, 0], up_weight[0, 0], down_weight[0, 0]]
    gain_row, router_t = (gain, router[0].T)
    partial = functools.partial
    block, message = shape((tokens, width)), shape((experts, slots, width))
    per_token = shape((experts, tokens), F32)

    def exchange(array, name, groups=None):
        with jax.named_scope(name):
            return lax.all_to_all(array, "expert", 0, 0, tiled=True, axis_index_groups=groups)

    def swap(pieces, name):
        return [piece if k == 0 else hop(piece, 0, k, name) for k, piece in enumerate(pieces)]

    half = lax.axis_size("expert") // 2
    me = lax.axis_index("expert").astype(jnp.int32).reshape(1)
    smem, vmem = pl.BlockSpec(memory_space=pltpu.SMEM), pl.BlockSpec(memory_space=pltpu.VMEM)
    xp = prev_input[0]
    xp_far = hop(xp, 0, half, "xp_far")
    dy_in = hop(next_cot[0], -1, 0, "dy_in")
    x_in = hop(next_input[0], 1, 0, "x_in")
    table = jnp.concatenate(
        [next_routes[0].T, prev_routes[0].T, next_priority, prev_priority], axis=0
    )
    far_table = hop(table, 0, half, "tables")

    def ranks(table, name):
        dims = shape((experts, tokens), jnp.int32)
        return call(partial(rank_kernel, capacity, top), name, [dims] * 2, [table])

    frank, rank = ranks(table, "ranks")
    piece, normed_scratch = shape((slots, width)), pltpu.VMEM((tokens, width), BF16)
    frank_far, rank_far = ranks(far_table, "far_ranks")
    longer_piece = shape((slots, width + LANES))

    def own_rows(x, batch, rank, name):
        extra = [per_token] + [block, shape((top, tokens), F32)] * batch
        outs = call(
            partial(own_kernel, half, batch, top),
            name,
            [longer_piece if batch else piece] * half + extra,
            [me, x, gain_row, router_t, table, rank],
            in_specs=[smem] + [vmem] * 5,
            scratch=[] if batch else [normed_scratch],
        )
        return swap(outs[:half], name), *outs[half:]

    def far_rows(x, batch, rank, name):
        outs = call(
            partial(far_kernel, half, batch, top),
            name,
            [longer_piece if batch else piece] * half,
            [me, x, gain_row, router_t, far_table, rank],
            in_specs=[smem] + [vmem] * 5,
            scratch=[normed_scratch, pltpu.VMEM((experts, tokens), F32)],
        )
        return swap(outs, name)

    own, _, normed, lifted = own_rows(xp, 1, rank, "own_rows")
    (cots,) = call(cots_kernel, "cots", [message], [rank, dy_in])
    cots = exchange(after(cots, xp_far, far_table, *own[1:]), "cots")
    far = far_rows(xp_far, 1, rank_far, "far_rows")
    frows, fweight = call(
        partial(rows_kernel, top),
        "frows",
        [message, per_token],
        [x_in, gain_row, router_t, table, frank],
        scratch=[normed_scratch],
    )
    frows = exchange(after(frows, cots, *far[1:]), "frows")

    count = experts * slots
    part = 256 if hidden % 256 == 0 else hidden
    columns = 512 if width % 512 == 0 else width
    steps = hidden // part
    grid = (steps + width // columns,)

    def whole(dims):
        return pl.BlockSpec(dims.shape, lambda i: (0,) * len(dims.shape), pipeline_mode=pl.Buffered(1))

    def early(i):
        return jnp.minimum(i, steps - 1)

    def late(i):
        return jnp.maximum(i - steps, 0)

    across_a = pl.BlockSpec((width, part), lambda i: (0, early(i)))
    down_a = pl.BlockSpec((part, width), lambda i: (early(i), 0))
    across_b = pl.BlockSpec((columns, hidden), lambda i: (late(i), 0))
    down_b = pl.BlockSpec((hidden, columns), lambda i: (0, late(i)))
    flops = 2 * count * width * hidden
    flat, hidden_shape = shape((count, width)), shape((steps, count, part))
    flat_longer = shape((count, width + LANES))
    grads, flat_rows, scaled, *parts = call(
        partial(expert_kernel, steps, half),
        "expert",
        [flat_longer, flat, flat] + [hidden_shape] * 3,
        [me] + mats + mats + [cots] + own + far,
        grid=grid,
        in_specs=[smem, across_a, across_a, down_a, across_b, across_b, down_b, whole(message)]
        + [whole(longer_piece)] * experts,
        out_specs=[whole(flat_longer)] + [whole(flat)] * 2 + [whole(hidden_shape)] * 3,
        scratch=[pltpu.VMEM((count, 1), F32)],
        flops=6 * flops,
    )
    active, gate_part, up_part = (jnp.swapaxes(a, 0, 1).reshape(count, hidden) for a in parts)
    grads = grads.reshape(experts, slots, width + LANES)
    grads = exchange(after(grads, frows), "grads")
    (outs,) = call(
        partial(forward_kernel, steps),
        "forward",
        [message],
        [frows] + mats,
        grid=grid,
        in_specs=[whole(message), across_a, across_a, down_b],
        out_specs=[pl.BlockSpec((experts, slots, columns), lambda i: (0, 0, late(i)))],
        scratch=[pltpu.VMEM(hidden_shape.shape, BF16)],
        flops=3 * flops,
    )
    gate_wgrad = t_dot(flat_rows, gate_part).astype(BF16)
    up_wgrad = t_dot(flat_rows, up_part).astype(BF16)
    down_wgrad = t_dot(active, scaled).astype(BF16)
    outs = exchange(after(outs, grads, gate_wgrad, up_wgrad, down_wgrad), "outs")

    grad_in, sums = call(
        partial(source_kernel, top),
        "source",
        [block, shape((-(-(experts + 1) // 8) * 8, width), F32)],
        [rank, grads, table, lifted, router_t, normed, xp, dy_in, gain_row],
        scratch=[
            pltpu.VMEM((count, tokens), BF16),
            pltpu.VMEM((experts, tokens), F32),
        ],
    )
    sums = swap([sums] * half, "sums")
    while len(sums) > 1:
        sums = [a + b for a, b in zip(sums[::2], sums[1::2])]
    sums = sums[0] + hop(sums[0], 0, half, "sums_far")
    (spread,) = call(
        partial(spread_kernel, slots),
        "spread",
        [shape((tokens, count))],
        [frank, fweight],
        scratch=[pltpu.VMEM((count, tokens), F32)],
    )
    forward = (x_in.astype(F32) + dot(spread, outs.reshape(count, width))).astype(BF16)
    return (
        forward[None],
        grad_in[None],
        gate_wgrad[None, None],
        up_wgrad[None, None],
        down_wgrad[None, None],
        sums[:experts].T[None],
        sums[experts][None],
    )


def solution(mesh):
    rows = P("pipe", "expert", None)
    weights = P("pipe", "expert", None, None)
    shared = P("pipe", None, None)
    return jax.shard_map(
        per_device,
        mesh=mesh,
        in_specs=(rows,) * 3
        + (weights,) * 3
        + (shared, P("pipe", None), rows, rows, P("pipe", "expert"), P("pipe", "expert")),
        out_specs=(rows, rows, weights, weights, weights, shared, P("pipe", None)),
        check_vma=False,
    )
```

```python
import functools

import jax
import jax.numpy as jnp
from jax import lax
from jax.experimental import pallas as pl
from jax.experimental.pallas import tpu as pltpu
from jax.sharding import PartitionSpec as P

EPS = 1e-06
F32 = jnp.float32
BF16 = jnp.bfloat16
VMEM_BYTES = 56 * 1024 * 1024
LANES = 128
SCALE = 64


def hop(block, pipe_step, flip, name):
    pipes, experts = lax.axis_size("pipe"), lax.axis_size("expert")
    with jax.named_scope(name):
        if pipe_step == 0:
            return lax.ppermute(block, "expert", [(e, e ^ flip) for e in range(experts)])
        route = [
            (p * experts + e, ((p + pipe_step) % pipes) * experts + (e ^ flip))
            for p in range(pipes)
            for e in range(experts)
        ]
        return lax.ppermute(block, ("pipe", "expert"), route)


def after(block, *earlier):
    return lax.optimization_barrier((block,) + earlier)[0]


def dot(a, b):
    return jnp.dot(a, b, preferred_element_type=F32)


def dot_t(a, b):
    return lax.dot_general(a, b, (((1,), (1,)), ((), ())), preferred_element_type=F32)


def t_dot(a, b, precision=None):
    dims = (((0,), (0,)), ((), ()))
    return lax.dot_general(a, b, dims, preferred_element_type=F32, precision=precision)


def iota(shape, dim):
    return lax.broadcasted_iota(jnp.int32, shape, dim)


def call(kernel, name, outs, ins, grid=(), in_specs=None, out_specs=None, scratch=(), flops=0):
    whole = pl.BlockSpec(memory_space=pltpu.VMEM)
    moved = sum(a.size * a.dtype.itemsize for a in list(outs) + list(ins))
    return pl.pallas_call(
        kernel,
        out_shape=[jax.ShapeDtypeStruct(o.shape, o.dtype) for o in outs],
        grid=grid,
        in_specs=in_specs or [whole] * len(ins),
        out_specs=out_specs or [whole] * len(outs),
        scratch_shapes=list(scratch),
        compiler_params=pltpu.CompilerParams(vmem_limit_bytes=VMEM_BYTES),
        cost_estimate=pl.CostEstimate(flops=flops // SCALE, bytes_accessed=moved // SCALE, transcendentals=0),
        name=name,
    )(*ins)


def shape(dims, dtype=BF16):
    return jax.ShapeDtypeStruct(tuple(dims), dtype)


def rank_kernel(capacity, top, table_ref, *rank_refs):
    experts, tokens = rank_refs[0].shape
    for batch, rank_ref in enumerate(rank_refs):
        row = 2 * top + batch
        order = jnp.broadcast_to(table_ref[row : row + 1, :], (tokens, tokens))
        before = (order.T < order).astype(F32).astype(BF16)
        chosen = iota((experts, tokens), 0) < 0
        for routes in route_rows(table_ref, batch, top):
            chosen = chosen | (routes == iota((experts, tokens), 0))
        count = dot(chosen.astype(F32).astype(BF16), before)
        rank_ref[...] = jnp.where(chosen & (count < capacity), count.astype(jnp.int32), -1)


def route_rows(ref, batch, top):
    return [ref[batch * top + j : batch * top + j + 1, :] for j in range(top)]


def slot_mask(rank_ref, e, slots):
    rank = rank_ref[e : e + 1, :]
    return iota((slots, rank.shape[1]), 0) == rank


def one_hot(mask):
    return jnp.where(mask, 1.0, 0.0).astype(BF16)


def normalise(x_ref, gain_ref, normed_ref, step=32):
    def part(i, carry):
        rows = pl.ds(pl.multiple_of(i * step, step), step)
        values = x_ref[rows, :].astype(F32)
        scale = lax.rsqrt(jnp.mean(values * values, axis=-1, keepdims=True) + EPS)
        normed_ref[rows, :] = (values * scale * gain_ref[...]).astype(BF16)
        return carry

    lax.fori_loop(0, x_ref.shape[0] // step, part, 0)


def gates(normed_ref, router_ref, routes, lifted_ref, weight_ref):
    logits = dot_t(router_ref[...], normed_ref[...])
    everyone = iota(logits.shape, 0)
    lifted = [
        jax.nn.sigmoid(jnp.sum(jnp.where(r == everyone, logits, 0.0), axis=0, keepdims=True))
        for r in routes
    ]
    total = functools.reduce(jnp.add, lifted)
    weight = jnp.zeros(weight_ref.shape, F32)
    for j, (r, value) in enumerate(zip(routes, lifted)):
        if lifted_ref is not None:
            lifted_ref[j : j + 1, :] = value
        weight = weight + jnp.where(r == everyone, value / total, 0.0)
    weight_ref[...] = weight


def put_pieces(me_ref, rank_ref, block_ref, weight_ref, pieces):
    width = block_ref.shape[1]
    for k, piece in enumerate(pieces):
        expert = pl.ds(me_ref[0] ^ k, 1)
        rank = rank_ref[expert, :]
        hot = one_hot(iota((piece.shape[0], rank.shape[1]), 0) == rank)
        piece[:, :width] = dot(hot, block_ref[...]).astype(BF16)
        if weight_ref is not None:
            weight = weight_ref[expert, :].astype(BF16)
            weight = jnp.broadcast_to(weight, (LANES, weight.shape[1]))
            piece[:, width:] = dot_t(hot, weight).astype(BF16)


def own_kernel(half, batch, top, *refs):
    me_ref, x_ref, gain_ref, router_ref, table_ref, rank_ref = refs[:6]
    pieces, (weight_ref, normed_ref, lifted_ref) = refs[6 : 6 + half], (*refs[6 + half :], None)[:3]
    normalise(x_ref, gain_ref, normed_ref)
    gates(normed_ref, router_ref, route_rows(table_ref, batch, top), lifted_ref, weight_ref)
    put_pieces(me_ref, rank_ref, normed_ref, weight_ref if batch else None, pieces)


def far_kernel(half, batch, top, *refs):
    me_ref, x_ref, gain_ref, router_ref, table_ref, rank_ref = refs[:6]
    pieces, (normed_ref, weight_ref) = refs[6 : 6 + half], refs[6 + half :]
    normalise(x_ref, gain_ref, normed_ref)
    if batch:
        gates(normed_ref, router_ref, route_rows(table_ref, batch, top), None, weight_ref)
    put_pieces(me_ref, rank_ref, normed_ref, weight_ref if batch else None, pieces)


def cots_kernel(rank_ref, x_ref, message_ref):
    for e in range(message_ref.shape[0]):
        hot = one_hot(slot_mask(rank_ref, e, message_ref.shape[1]))
        message_ref[e] = dot(hot, x_ref[...]).astype(BF16)


def flat_of(ref):
    return ref[...].reshape(-1, ref.shape[-1])


def each_sender(me_ref, count, slots):
    for k in range(count):
        sender = me_ref[0] ^ k
        yield k, sender, pl.ds(pl.multiple_of(sender * slots, 16), slots)


def expert_kernel(steps, half, *refs):
    me_ref, gate_a, up_a, down_a, gate_b, up_b, down_b, cot_ref = refs[:8]
    pieces, refs = refs[8 : 8 + 2 * half], refs[8 + 2 * half :]
    message_ref, rows_ref, scaled_ref, active_ref, gate_part_ref, up_part_ref, inner_ref = refs
    slots = pieces[0].shape[0]
    width = rows_ref.shape[1]
    step = pl.program_id(0)

    @pl.when(step == 0)
    def _():
        for k, sender, part in each_sender(me_ref, 2 * half, slots):
            rows_ref[part, :] = pieces[k][:, :width]
            scale = pieces[k][:, width:].astype(F32)[:, :1]
            scaled_ref[part, :] = (scale * cot_ref[sender].astype(F32)).astype(BF16)
        inner_ref[...] = jnp.zeros_like(inner_ref)

    @pl.when(step < steps)
    def _():
        gate = dot(rows_ref[...], gate_a[...])
        upper = dot(rows_ref[...], up_a[...])
        sig = jax.nn.sigmoid(gate)
        act_grad = dot_t(scaled_ref[...], down_a[...])
        active_ref[step] = (gate * sig * upper).astype(BF16)
        gate_part_ref[step] = (act_grad * upper * sig * (1.0 + gate * (1.0 - sig))).astype(BF16)
        up_part_ref[step] = (act_grad * (gate * sig)).astype(BF16)

    @pl.when(step >= steps)
    def _():
        part = gate_a.shape[1]
        columns = pl.ds(pl.multiple_of((step - steps) * gate_b.shape[0], 128), gate_b.shape[0])
        total = jnp.zeros((rows_ref.shape[0], gate_b.shape[0]), F32)
        result = total
        for f in range(steps):
            hidden = slice(f * part, (f + 1) * part)
            total = total + dot_t(gate_part_ref[f], gate_b[:, hidden])
            total = total + dot_t(up_part_ref[f], up_b[:, hidden])
            result = result + dot(active_ref[f], down_b[hidden, :])
        message_ref[:, columns] = total.astype(BF16)
        cot = cot_ref[:, :, columns].reshape(total.shape).astype(F32)
        result = result.astype(BF16).astype(F32)
        inner_ref[...] += jnp.sum(cot * result, axis=1, keepdims=True)

    @pl.when(step == pl.num_programs(0) - 1)
    def _():
        inner = inner_ref[...].astype(BF16)
        message_ref[:, width:] = jnp.broadcast_to(inner, (inner.shape[0], LANES))


def forward_kernel(half, me_ref, gate_w, up_w, down_w, *refs):
    pieces, (out_ref, rows_ref) = refs[:half], refs[-2:]
    slots = pieces[0].shape[0]
    for k, piece in enumerate(pieces):
        start = pl.multiple_of((me_ref[0] ^ k) % half * slots, 16)
        rows_ref[pl.ds(start, slots), :] = piece[...]
    gate = dot(rows_ref[...], gate_w[...])
    active = (gate * jax.nn.sigmoid(gate) * dot(rows_ref[...], up_w[...])).astype(BF16)
    columns = 512 if out_ref.shape[2] % 512 == 0 else out_ref.shape[2]
    for c in range(0, out_ref.shape[2], columns):
        result = dot(active, down_w[:, c : c + columns]).astype(BF16)
        out_ref[:, :, c : c + columns] = result.reshape(half, slots, columns)


def spread_kernel(slots, rank_ref, weight_ref, spread_ref, flat_ref):
    for e in range(rank_ref.shape[0]):
        mask = slot_mask(rank_ref, e, slots)
        flat_ref[e * slots : (e + 1) * slots, :] = jnp.where(mask, weight_ref[e : e + 1, :], 0.0)
    spread_ref[...] = flat_ref[...].T.astype(BF16)


def split(value):
    parts = []
    for _ in range(3):
        parts.append(value.astype(BF16).astype(F32))
        value = value - parts[-1]
    return jnp.concatenate(parts, axis=0).astype(BF16)


def bare_of(x_ref):
    values = x_ref[...].astype(F32)
    scale = lax.rsqrt(jnp.mean(values * values, axis=-1, keepdims=True) + EPS)
    return values * scale, scale


def sums_kernel(top, cuts, *refs):
    rank_ref, hot_ref, table_ref, lifted_ref, router_ref, normed_ref, xp_ref = refs[:7]
    grads, (dnormed_ref, sums_ref, terms_ref) = refs[7 : 7 + cuts], refs[7 + cuts :]
    experts, tokens = rank_ref.shape
    some, slots, _ = grads[0].shape
    width = xp_ref.shape[1]
    for e in range(experts):
        hot = one_hot(slot_mask(rank_ref, e, slots))
        terms_ref[e : e + 1, :] = t_dot(grads[e // some][e % some, :, width:], hot)[:1, :]
    routes = route_rows(table_ref, 1, top)
    everyone = iota((experts, tokens), 0)
    lifted = [lifted_ref[j : j + 1, :] for j in range(top)]
    dweight = [
        jnp.sum(jnp.where(r == everyone, terms_ref[...], 0.0), axis=0, keepdims=True)
        for r in routes
    ]
    total = functools.reduce(jnp.add, lifted)
    both = functools.reduce(jnp.add, [d * l for d, l in zip(dweight, lifted)])
    dlogits = jnp.zeros((experts, tokens), F32)
    for r, d, l in zip(routes, dweight, lifted):
        dsel = (d / total - both / (total * total)) * l * (1.0 - l)
        dlogits = dlogits + jnp.where(r == everyone, dsel, 0.0)
    stacked = split(dlogits)
    terms = dot(stacked, normed_ref[...])
    sums_ref[...] = jnp.zeros_like(sums_ref)
    sums_ref[:experts, :] = terms[:experts] + (terms[experts : 2 * experts] + terms[2 * experts :])
    router = jnp.concatenate([router_ref[...].astype(F32)] * 3, axis=0).astype(BF16)
    dnormed = t_dot(stacked, router)
    for c, ref in enumerate(grads):
        part = slice(c * some * slots, (c + 1) * some * slots)
        dnormed = dnormed + dot(hot_ref[:, part], ref[:, :, :width].reshape(-1, width))
    dnormed_ref[...] = dnormed
    gain_sum = jnp.sum(dnormed * bare_of(xp_ref)[0], axis=0, keepdims=True)
    sums_ref[experts : experts + 1, :] = gain_sum


def source_kernel(dnormed_ref, xp_ref, dy_ref, gain_ref, grad_ref):
    bare, scale = bare_of(xp_ref)
    lifted_grad = dnormed_ref[...] * gain_ref[...]
    slope = jnp.mean(lifted_grad * bare, axis=-1, keepdims=True)
    grad_ref[...] = (dy_ref[...].astype(F32) + scale * (lifted_grad - bare * slope)).astype(BF16)


def per_device(
    next_input,
    prev_input,
    next_cot,
    gate_weight,
    up_weight,
    down_weight,
    router,
    gain,
    next_routes,
    prev_routes,
    next_priority,
    prev_priority,
):
    experts = router.shape[-1]
    tokens, width = next_input.shape[1:]
    hidden = gate_weight.shape[-1]
    top = next_routes.shape[-1]
    capacity = (5 * top * tokens + 4 * experts - 1) // (4 * experts)
    slots = -(-capacity // 16) * 16
    mats = [gate_weight[0, 0], up_weight[0, 0], down_weight[0, 0]]
    gain_row, router_t = (gain, router[0].T)
    partial = functools.partial
    block, message = shape((tokens, width)), shape((experts, slots, width))
    per_token = shape((experts, tokens), F32)

    def exchange(array, name, groups=None):
        with jax.named_scope(name):
            return lax.all_to_all(array, "expert", 0, 0, tiled=True, axis_index_groups=groups)

    def swap(pieces, name):
        return [piece if k == 0 else hop(piece, 0, k, name) for k, piece in enumerate(pieces)]

    half = lax.axis_size("expert") // 2
    me = lax.axis_index("expert").astype(jnp.int32).reshape(1)
    smem, vmem = pl.BlockSpec(memory_space=pltpu.SMEM), pl.BlockSpec(memory_space=pltpu.VMEM)
    xp = prev_input[0]
    xp_far = hop(xp, 0, half, "xp_far")
    dy_in = hop(next_cot[0], -1, 0, "dy_in")
    x_in = hop(next_input[0], 1, 0, "x_in")
    table = jnp.concatenate(
        [next_routes[0].T, prev_routes[0].T, next_priority, prev_priority], axis=0
    )
    far_table = hop(table, 0, half, "tables")

    def ranks(table, name):
        dims = shape((experts, tokens), jnp.int32)
        return call(partial(rank_kernel, capacity, top), name, [dims] * 2, [table])

    frank, rank = ranks(table, "ranks")
    piece, normed_scratch = shape((slots, width)), pltpu.VMEM((tokens, width), BF16)
    frank_far, rank_far = ranks(far_table, "far_ranks")
    longer_piece = shape((slots, width + LANES))

    def own_rows(x, batch, rank, name):
        extra = [per_token] + [block, shape((top, tokens), F32)] * batch
        outs = call(
            partial(own_kernel, half, batch, top),
            name,
            [longer_piece if batch else piece] * half + extra,
            [me, x, gain_row, router_t, table, rank],
            in_specs=[smem] + [vmem] * 5,
            scratch=[] if batch else [normed_scratch],
        )
        return swap(outs[:half], name), *outs[half:]

    def far_rows(x, batch, rank, name):
        outs = call(
            partial(far_kernel, half, batch, top),
            name,
            [longer_piece if batch else piece] * half,
            [me, x, gain_row, router_t, far_table, rank],
            in_specs=[smem] + [vmem] * 5,
            scratch=[normed_scratch, pltpu.VMEM((experts, tokens), F32)],
        )
        return swap(outs, name)

    own, _, normed, lifted = own_rows(xp, 1, rank, "own_rows")
    (cots,) = call(cots_kernel, "cots", [message], [rank, dy_in])
    cots = exchange(after(cots, xp_far, far_table, *own[1:]), "cots")
    far = far_rows(xp_far, 1, rank_far, "far_rows")
    x_far = hop(after(next_input[0], cots, *far[1:]), 1, half, "x_far")
    fown, fweight = own_rows(x_in, 0, frank, "fown_rows")
    ffar = far_rows(x_far, 0, frank_far, "ffar_rows")

    count = experts * slots
    part = 256 if hidden % 256 == 0 else hidden
    columns = 512 if width % 512 == 0 else width
    steps = hidden // part
    grid = (steps + width // columns,)

    def whole(dims):
        return pl.BlockSpec(dims.shape, lambda *_: (0,) * len(dims.shape), pipeline_mode=pl.Buffered(1))

    def early(i):
        return jnp.minimum(i, steps - 1)

    def late(i):
        return jnp.maximum(i - steps, 0)

    across_a = pl.BlockSpec((width, part), lambda i, *_: (0, early(i)))
    down_a = pl.BlockSpec((part, width), lambda i: (early(i), 0))
    across_b = pl.BlockSpec((columns, hidden), lambda i: (late(i), 0))
    down_b = pl.BlockSpec((hidden, columns), lambda i, *_: (0, late(i)))
    flops = 2 * count * width * hidden
    def spread_of(rank, weight, name):
        return call(
            partial(spread_kernel, slots),
            name,
            [shape((tokens, count))],
            [rank, weight],
            scratch=[pltpu.VMEM((count, tokens), F32)],
        )[0]

    spread = spread_of(frank, fweight, "spread")
    hot = spread_of(rank, jnp.ones((experts, tokens), F32), "hot")
    flat, hidden_shape = shape((count, width)), shape((steps, count, part))
    flat_longer = shape((count, width + LANES))
    grads, flat_rows, scaled, *parts = call(
        partial(expert_kernel, steps, half),
        "expert",
        [flat_longer, flat, flat] + [hidden_shape] * 3,
        [me] + mats + mats + [cots] + own + far,
        grid=grid,
        in_specs=[smem, across_a, across_a, down_a, across_b, across_b, down_b, whole(message)]
        + [whole(longer_piece)] * experts,
        out_specs=[whole(flat_longer)] + [whole(flat)] * 2 + [whole(hidden_shape)] * 3,
        scratch=[pltpu.VMEM((count, 1), F32)],
        flops=6 * flops,
    )
    active, gate_part, up_part = (jnp.swapaxes(a, 0, 1).reshape(count, hidden) for a in parts)
    grads = grads.reshape(experts, slots, width + LANES)
    grads = exchange(after(grads, x_far, hot, spread, *fown[1:]), "grads")

    def forward_of(pieces, flip, name, *filled):
        return pl.pallas_call(
            partial(forward_kernel, half),
            out_shape=message,
            grid_spec=pltpu.PrefetchScalarGridSpec(
                num_scalar_prefetch=1,
                grid=(1,),
                in_specs=[whole(m) for m in mats]
                + [whole(piece)] * half
                + [pl.BlockSpec(memory_space=pl.ANY)] * len(filled),
                out_specs=pl.BlockSpec(
                    (half, slots, width), lambda i, me_ref: (me_ref[0] // half ^ flip, 0, 0)
                ),
                scratch_shapes=[pltpu.VMEM((count // 2, width), BF16)],
            ),
            input_output_aliases={4 + half: 0} if filled else {},
            compiler_params=pltpu.CompilerParams(vmem_limit_bytes=VMEM_BYTES),
            cost_estimate=pl.CostEstimate(
                flops=3 * flops // 2, bytes_accessed=6 * width * hidden, transcendentals=0
            ),
            name=name,
        )(me, *mats, *pieces, *filled)

    outs = forward_of(fown, 0, "forward_own")
    outs = forward_of(ffar, 1, "forward_far", outs)
    outs = exchange(after(outs, grads), "outs")

    cuts = 4 if experts % 4 == 0 else 1
    sums_shape = shape((-(-(experts + 1) // 8) * 8, width), F32)

    def full(array):
        return pl.BlockSpec(array.shape, lambda i: (0,) * len(array.shape))

    def cut_at(c):
        return pl.BlockSpec((experts // cuts, slots, width + LANES), lambda i: (c, 0, 0))

    known = [rank, hot, table, lifted, router_t, normed, xp]
    dnormed, sums = call(
        partial(sums_kernel, top, cuts),
        "sums",
        [shape((tokens, width), F32), sums_shape],
        known + [grads] * cuts,
        grid=(1,),
        in_specs=[full(a) for a in known] + [cut_at(c) for c in range(cuts)],
        out_specs=[full(shape((tokens, width))), full(sums_shape)],
        scratch=[pltpu.VMEM((experts, tokens), F32)],
    )
    flat_rows, active = after((flat_rows, active), sums)
    gate_wgrad = t_dot(flat_rows, gate_part).astype(BF16)
    up_wgrad = t_dot(flat_rows, up_part).astype(BF16)
    down_wgrad = t_dot(active, scaled).astype(BF16)
    sums = swap([sums] * half, "sums")
    while len(sums) > 1:
        sums = [a + b for a, b in zip(sums[::2], sums[1::2])]
    far_sums = hop(sums[0], 0, half, "sums_far")
    (grad_in,) = call(source_kernel, "source", [block], [dnormed, xp, dy_in, gain_row])
    forward = (x_in.astype(F32) + dot(spread, outs.reshape(count, width))).astype(BF16)
    far_sums, forward = lax.optimization_barrier((far_sums, forward))
    sums = sums[0] + far_sums
    return (
        forward[None],
        grad_in[None],
        gate_wgrad[None, None],
        up_wgrad[None, None],
        down_wgrad[None, None],
        sums[:experts].T[None],
        sums[experts][None],
    )


def solution(mesh):
    rows = P("pipe", "expert", None)
    weights = P("pipe", "expert", None, None)
    shared = P("pipe", None, None)
    return jax.shard_map(
        per_device,
        mesh=mesh,
        in_specs=(rows,) * 3
        + (weights,) * 3
        + (shared, P("pipe", None), rows, rows, P("pipe", "expert"), P("pipe", "expert")),
        out_specs=(rows, rows, weights, weights, weights, shared, P("pipe", None)),
        check_vma=False,
    )
```

```python
import functools

import jax
import jax.numpy as jnp
from jax import lax
from jax.experimental import pallas as pl
from jax.experimental.pallas import tpu as pltpu
from jax.sharding import PartitionSpec as P

EPS = 1e-06
F32 = jnp.float32
BF16 = jnp.bfloat16
VMEM_BYTES = 56 * 1024 * 1024
LANES = 128
SCALE = 64


def hop(block, pipe_step, flip, name):
    pipes, experts = lax.axis_size("pipe"), lax.axis_size("expert")
    with jax.named_scope(name):
        if pipe_step == 0:
            return lax.ppermute(block, "expert", [(e, e ^ flip) for e in range(experts)])
        route = [
            (p * experts + e, ((p + pipe_step) % pipes) * experts + (e ^ flip))
            for p in range(pipes)
            for e in range(experts)
        ]
        return lax.ppermute(block, ("pipe", "expert"), route)


def after(block, *earlier):
    return lax.optimization_barrier((block,) + earlier)[0]


def dot(a, b):
    return jnp.dot(a, b, preferred_element_type=F32)


def dot_t(a, b):
    return lax.dot_general(a, b, (((1,), (1,)), ((), ())), preferred_element_type=F32)


def t_dot(a, b, precision=None):
    dims = (((0,), (0,)), ((), ()))
    return lax.dot_general(a, b, dims, preferred_element_type=F32, precision=precision)


def iota(shape, dim):
    return lax.broadcasted_iota(jnp.int32, shape, dim)


def call(kernel, name, outs, ins, grid=(), in_specs=None, out_specs=None, scratch=(), flops=0):
    whole = pl.BlockSpec(memory_space=pltpu.VMEM)
    moved = sum(a.size * a.dtype.itemsize for a in list(outs) + list(ins))
    return pl.pallas_call(
        kernel,
        out_shape=[jax.ShapeDtypeStruct(o.shape, o.dtype) for o in outs],
        grid=grid,
        in_specs=in_specs or [whole] * len(ins),
        out_specs=out_specs or [whole] * len(outs),
        scratch_shapes=list(scratch),
        compiler_params=pltpu.CompilerParams(vmem_limit_bytes=VMEM_BYTES),
        cost_estimate=pl.CostEstimate(flops=flops // SCALE, bytes_accessed=moved // SCALE, transcendentals=0),
        name=name,
    )(*ins)


def shape(dims, dtype=BF16):
    return jax.ShapeDtypeStruct(tuple(dims), dtype)


def rank_kernel(capacity, top, table_ref, *rank_refs):
    experts, tokens = rank_refs[0].shape
    for batch, rank_ref in enumerate(rank_refs):
        row = 2 * top + batch
        order = jnp.broadcast_to(table_ref[row : row + 1, :], (tokens, tokens))
        before = (order.T < order).astype(F32).astype(BF16)
        chosen = iota((experts, tokens), 0) < 0
        for routes in route_rows(table_ref, batch, top):
            chosen = chosen | (routes == iota((experts, tokens), 0))
        count = dot(chosen.astype(F32).astype(BF16), before)
        rank_ref[...] = jnp.where(chosen & (count < capacity), count.astype(jnp.int32), -1)


def route_rows(ref, batch, top):
    return [ref[batch * top + j : batch * top + j + 1, :] for j in range(top)]


def slot_mask(rank_ref, e, slots):
    rank = rank_ref[e : e + 1, :]
    return iota((slots, rank.shape[1]), 0) == rank


def one_hot(mask):
    return jnp.where(mask, 1.0, 0.0).astype(BF16)


def normalise(x_ref, gain_ref, normed_ref, step=32):
    def part(i, carry):
        rows = pl.ds(pl.multiple_of(i * step, step), step)
        values = x_ref[rows, :].astype(F32)
        scale = lax.rsqrt(jnp.mean(values * values, axis=-1, keepdims=True) + EPS)
        normed_ref[rows, :] = (values * scale * gain_ref[...]).astype(BF16)
        return carry

    lax.fori_loop(0, x_ref.shape[0] // step, part, 0)


def sigmoids(normed_ref, router_ref, routes):
    logits = dot_t(router_ref[...], normed_ref[...])
    everyone = iota(logits.shape, 0)
    picked = [jnp.sum(jnp.where(r == everyone, logits, 0.0), axis=0, keepdims=True) for r in routes]
    return [jax.nn.sigmoid(value) for value in picked]


def side_of(expert, experts, routes, lifted):
    tokens = routes[0].shape[1]
    everyone = iota((experts, tokens), 0)
    total = functools.reduce(jnp.add, lifted)
    slope = jnp.zeros((experts, tokens), F32)
    mine = jnp.zeros((1, tokens), F32)
    for r, value in zip(routes, lifted):
        slope = slope + jnp.where(r == everyone, value * (1.0 - value), 0.0)
        mine = mine + jnp.where(r == expert, value, 0.0)
    acts = slope * (jnp.where(everyone == expert, 1.0 / total, 0.0) - mine / (total * total))
    high = acts.astype(BF16).astype(F32)
    weight = jnp.broadcast_to(mine / total, (LANES - 2 * experts, tokens))
    return jnp.concatenate([high, acts - high, weight], axis=0).astype(BF16)


def put_pieces(me_ref, rank_ref, block_ref, pieces, routes=None, lifted=None):
    width = block_ref.shape[1]
    for k, piece in enumerate(pieces):
        expert = me_ref[0] ^ k
        rank = rank_ref[pl.ds(expert, 1), :]
        hot = one_hot(iota((piece.shape[0], rank.shape[1]), 0) == rank)
        piece[:, :width] = dot(hot, block_ref[...]).astype(BF16)
        if lifted:
            side = side_of(expert, rank_ref.shape[0], routes, lifted)
            piece[:, width:] = dot_t(hot, side).astype(BF16)


def back_rows_kernel(half, top, *refs):
    me_ref, x_ref, gain_ref, router_ref, table_ref, rank_ref = refs[:6]
    pieces, normed_ref = refs[6:-1], refs[-1]
    normalise(x_ref, gain_ref, normed_ref)
    routes = route_rows(table_ref, 1, top)
    lifted = sigmoids(normed_ref, router_ref, routes)
    put_pieces(me_ref, rank_ref, normed_ref, pieces, routes, lifted)


def next_rows_kernel(half, top, *refs):
    me_ref, x_ref, gain_ref, router_ref, table_ref, rank_ref = refs[:6]
    pieces, weight_ref, normed_ref = refs[6 : 6 + half], refs[6 + half], refs[-1]
    normalise(x_ref, gain_ref, normed_ref)
    put_pieces(me_ref, rank_ref, normed_ref, pieces)
    routes = route_rows(table_ref, 0, top)
    lifted = sigmoids(normed_ref, router_ref, routes)
    total = functools.reduce(jnp.add, lifted)
    weight = jnp.zeros(weight_ref.shape, F32)
    for r, value in zip(routes, lifted):
        weight = weight + jnp.where(r == iota(weight.shape, 0), value / total, 0.0)
    weight_ref[...] = weight


def cots_kernel(rank_ref, x_ref, message_ref):
    for e in range(message_ref.shape[0]):
        hot = one_hot(slot_mask(rank_ref, e, message_ref.shape[1]))
        message_ref[e] = dot(hot, x_ref[...]).astype(BF16)


def flat_of(ref):
    return ref[...].reshape(-1, ref.shape[-1])


def each_sender(me_ref, count, slots):
    for k in range(count):
        sender = me_ref[0] ^ k
        yield k, sender, pl.ds(pl.multiple_of(sender * slots, 16), slots)


def expert_kernel(steps, blocks, half, *refs):
    me_ref, gate_a, up_a, down_a, gate_b, up_b, down_b, router_ref, gain_ref, cot_ref = refs[:10]
    pieces, refs = refs[10 : 10 + 2 * half], refs[10 + 2 * half :]
    message_ref, rows_ref, scaled_ref, active_ref, gate_part_ref, up_part_ref, sums_ref = refs[:7]
    side_ref, inner_ref, high_ref, low_ref = refs[7:]
    slots, columns, part = pieces[0].shape[0], gate_b.shape[0], gate_a.shape[1]
    count, width = rows_ref.shape
    experts = router_ref.shape[0]
    step = pl.program_id(0)

    def span_of(first):
        return pl.ds(pl.multiple_of((step - first) * columns, 128), columns)

    @pl.when(step == 0)
    def _():
        for k, sender, rows in each_sender(me_ref, 2 * half, slots):
            rows_ref[rows, :] = pieces[k][:, :width]
            side = pieces[k][:, width:]
            side_ref[rows, :] = side
            scale = side.astype(F32)[:, LANES - 1 :]
            scaled_ref[rows, :] = (scale * cot_ref[sender].astype(F32)).astype(BF16)
        inner_ref[...] = jnp.zeros_like(inner_ref)
        sums_ref[...] = jnp.zeros_like(sums_ref)

    @pl.when(step < steps)
    def _():
        gate = dot(rows_ref[...], gate_a[...])
        upper = dot(rows_ref[...], up_a[...])
        sig = jax.nn.sigmoid(gate)
        act_grad = dot_t(scaled_ref[...], down_a[...])
        active_ref[step] = (gate * sig * upper).astype(BF16)
        gate_part_ref[step] = (act_grad * upper * sig * (1.0 + gate * (1.0 - sig))).astype(BF16)
        up_part_ref[step] = (act_grad * (gate * sig)).astype(BF16)

    @pl.when((step >= steps) & (step < steps + blocks))
    def _():
        result = jnp.zeros((count, columns), F32)
        for f in range(steps):
            result = result + dot(active_ref[f], down_b[f * part : (f + 1) * part, :])
        cot = cot_ref[:, :, span_of(steps)].reshape(count, columns).astype(F32)
        result = result.astype(BF16).astype(F32)
        inner_ref[...] += jnp.sum(cot * result, axis=1, keepdims=True)

    @pl.when(step == steps + blocks)
    def _():
        terms = inner_ref[...].astype(BF16).astype(F32) * side_ref[...].astype(F32)
        high_ref[...] = terms.astype(BF16)
        low_ref[...] = (terms - terms.astype(BF16).astype(F32)).astype(BF16)

    @pl.when(step >= steps + blocks)
    def _():
        span = span_of(steps + blocks)
        rows = rows_ref[:, span]
        router = router_ref[:, span].astype(F32)
        rest = jnp.zeros((LANES - 2 * experts, columns), F32)
        router = jnp.concatenate([router, router, rest], axis=0).astype(BF16)
        total = dot(high_ref[...], router) + dot(low_ref[...], router)
        for f in range(steps):
            units = slice(f * part, (f + 1) * part)
            total = total + dot_t(gate_part_ref[f], gate_b[:, units])
            total = total + dot_t(up_part_ref[f], up_b[:, units])
        message_ref[:, span] = total.astype(BF16)
        terms = t_dot(high_ref[...], rows) + t_dot(low_ref[...], rows)
        sums_ref[:experts, span] = terms[:experts] + terms[experts : 2 * experts]
        gain_sum = jnp.sum(total * rows.astype(F32), axis=0, keepdims=True)
        sums_ref[experts : experts + 1, span] = gain_sum / gain_ref[:, span]


def forward_kernel(half, me_ref, gate_w, up_w, down_w, *refs):
    pieces, (out_ref, rows_ref) = refs[:half], refs[-2:]
    slots = pieces[0].shape[0]
    for k, piece in enumerate(pieces):
        start = pl.multiple_of((me_ref[0] ^ k) % half * slots, 16)
        rows_ref[pl.ds(start, slots), :] = piece[...]
    gate = dot(rows_ref[...], gate_w[...])
    active = (gate * jax.nn.sigmoid(gate) * dot(rows_ref[...], up_w[...])).astype(BF16)
    columns = 512 if out_ref.shape[2] % 512 == 0 else out_ref.shape[2]
    for c in range(0, out_ref.shape[2], columns):
        result = dot(active, down_w[:, c : c + columns]).astype(BF16)
        out_ref[:, :, c : c + columns] = result.reshape(half, slots, columns)


def spread_kernel(slots, rank_ref, weight_ref, spread_ref, flat_ref):
    for e in range(rank_ref.shape[0]):
        mask = slot_mask(rank_ref, e, slots)
        flat_ref[e * slots : (e + 1) * slots, :] = jnp.where(mask, weight_ref[e : e + 1, :], 0.0)
    spread_ref[...] = flat_ref[...].T.astype(BF16)


def source_kernel(hot_ref, xp_ref, dy_ref, gain_ref, *refs):
    grads, grad_ref = refs[:-1], refs[-1]
    dnormed = jnp.zeros(xp_ref.shape, F32)
    for c, ref in enumerate(grads):
        rows = flat_of(ref)
        part = slice(c * rows.shape[0], (c + 1) * rows.shape[0])
        dnormed = dnormed + dot(hot_ref[:, part], rows)
    values = xp_ref[...].astype(F32)
    scale = lax.rsqrt(jnp.mean(values * values, axis=-1, keepdims=True) + EPS)
    bare = values * scale
    lifted_grad = dnormed * gain_ref[...]
    slope = jnp.mean(lifted_grad * bare, axis=-1, keepdims=True)
    grad_ref[...] = (dy_ref[...].astype(F32) + scale * (lifted_grad - bare * slope)).astype(BF16)


def per_device(
    next_input,
    prev_input,
    next_cot,
    gate_weight,
    up_weight,
    down_weight,
    router,
    gain,
    next_routes,
    prev_routes,
    next_priority,
    prev_priority,
):
    experts = router.shape[-1]
    tokens, width = next_input.shape[1:]
    hidden = gate_weight.shape[-1]
    top = next_routes.shape[-1]
    capacity = (5 * top * tokens + 4 * experts - 1) // (4 * experts)
    slots = -(-capacity // 16) * 16
    mats = [gate_weight[0, 0], up_weight[0, 0], down_weight[0, 0]]
    gain_row, router_t = (gain, router[0].T)
    partial = functools.partial
    block, message = shape((tokens, width)), shape((experts, slots, width))
    per_token = shape((experts, tokens), F32)

    def exchange(array, name, groups=None):
        with jax.named_scope(name):
            return lax.all_to_all(array, "expert", 0, 0, tiled=True, axis_index_groups=groups)

    def swap(pieces, name):
        return [piece if k == 0 else hop(piece, 0, k, name) for k, piece in enumerate(pieces)]

    half = lax.axis_size("expert") // 2
    me = lax.axis_index("expert").astype(jnp.int32).reshape(1)
    smem, vmem = pl.BlockSpec(memory_space=pltpu.SMEM), pl.BlockSpec(memory_space=pltpu.VMEM)
    xp = prev_input[0]
    xp_far = hop(xp, 0, half, "xp_far")
    dy_in = hop(next_cot[0], -1, 0, "dy_in")
    x_in = hop(next_input[0], 1, 0, "x_in")
    table = jnp.concatenate(
        [next_routes[0].T, prev_routes[0].T, next_priority, prev_priority], axis=0
    )
    far_table = hop(table, 0, half, "tables")

    def ranks(table, name):
        dims = shape((experts, tokens), jnp.int32)
        return call(partial(rank_kernel, capacity, top), name, [dims] * 2, [table])

    frank, rank = ranks(table, "ranks")
    piece, normed_scratch = shape((slots, width)), pltpu.VMEM((tokens, width), BF16)
    frank_far, rank_far = ranks(far_table, "far_ranks")
    longer_piece = shape((slots, width + LANES))

    def back_rows(x, table, rank, name):
        pieces = call(
            partial(back_rows_kernel, half, top),
            name,
            [longer_piece] * half,
            [me, x, gain_row, router_t, table, rank],
            in_specs=[smem] + [vmem] * 5,
            scratch=[normed_scratch],
        )
        return swap(pieces, name)

    def next_rows(x, table, rank, name):
        outs = call(
            partial(next_rows_kernel, half, top),
            name,
            [piece] * half + [per_token],
            [me, x, gain_row, router_t, table, rank],
            in_specs=[smem] + [vmem] * 5,
            scratch=[normed_scratch],
        )
        return swap(outs[:half], name), outs[0], outs[half]

    own = back_rows(xp, table, rank, "own_rows")
    (cots,) = call(cots_kernel, "cots", [message], [rank, dy_in])
    cots = exchange(after(cots, xp_far, far_table, *own[1:]), "cots")
    far = back_rows(xp_far, far_table, rank_far, "far_rows")
    x_far = hop(after(next_input[0], cots, *far[1:]), 1, half, "x_far")
    fown, _, fweight = next_rows(x_in, table, frank, "fown_rows")
    ffar, ffar_sent, _ = next_rows(x_far, far_table, frank_far, "ffar_rows")

    count = experts * slots
    part = 256 if hidden % 256 == 0 else hidden
    columns = 512 if width % 512 == 0 else width
    steps = hidden // part
    blocks = width // columns
    grid = (steps + 2 * blocks,)

    def whole(dims):
        return pl.BlockSpec(dims.shape, lambda *_: (0,) * len(dims.shape), pipeline_mode=pl.Buffered(1))

    def early(i):
        return jnp.minimum(i, steps - 1)

    def middle(i):
        return jnp.clip(i - steps, 0, blocks - 1)

    def late(i):
        return jnp.maximum(i - steps - blocks, 0)

    across_a = pl.BlockSpec((width, part), lambda i, *_: (0, early(i)))
    down_a = pl.BlockSpec((part, width), lambda i: (early(i), 0))
    across_b = pl.BlockSpec((columns, hidden), lambda i: (late(i), 0))
    down_b = pl.BlockSpec((hidden, columns), lambda i, *_: (0, middle(i)))
    flops = 2 * count * width * hidden
    def spread_of(rank, weight, name):
        return call(
            partial(spread_kernel, slots),
            name,
            [shape((tokens, count))],
            [rank, weight],
            scratch=[pltpu.VMEM((count, tokens), F32)],
        )[0]

    spread = spread_of(frank, fweight, "spread")
    hot = spread_of(rank, jnp.ones((experts, tokens), F32), "hot")
    flat, hidden_shape = shape((count, width)), shape((steps, count, part))
    sums_shape = shape((-(-(experts + 1) // 8) * 8, width), F32)
    grads, flat_rows, scaled, active, gate_part, up_part, sums = call(
        partial(expert_kernel, steps, blocks, half),
        "expert",
        [flat] * 3 + [hidden_shape] * 3 + [sums_shape],
        [me] + mats + mats + [router_t, gain_row, cots] + own + far,
        grid=grid,
        in_specs=[smem, across_a, across_a, down_a, across_b, across_b, down_b]
        + [whole(router_t), whole(gain_row), whole(message)]
        + [whole(longer_piece)] * experts,
        out_specs=[whole(flat)] * 3 + [whole(hidden_shape)] * 3 + [whole(sums_shape)],
        scratch=[
            pltpu.VMEM((count, LANES), BF16),
            pltpu.VMEM((count, 1), F32),
            pltpu.VMEM((count, LANES), BF16),
            pltpu.VMEM((count, LANES), BF16),
        ],
        flops=6 * flops,
    )
    active, gate_part, up_part = (
        jnp.swapaxes(a, 0, 1).reshape(count, hidden) for a in (active, gate_part, up_part)
    )
    grads = grads.reshape(experts, slots, width)
    grads = exchange(after(grads, x_far, hot, spread, *fown[1:]), "grads")
    flat_rows, active = after((flat_rows, active), ffar_sent)
    gate_wgrad = t_dot(flat_rows, gate_part).astype(BF16)
    up_wgrad = t_dot(flat_rows, up_part).astype(BF16)
    down_wgrad = t_dot(active, scaled).astype(BF16)
    packed = [sums[:experts], sums[experts].reshape(experts, width // experts)]
    packed = jnp.concatenate(packed, axis=1)

    def forward_of(pieces, flip, name, *filled):
        return pl.pallas_call(
            partial(forward_kernel, half),
            out_shape=message,
            grid_spec=pltpu.PrefetchScalarGridSpec(
                num_scalar_prefetch=1,
                grid=(1,),
                in_specs=[whole(m) for m in mats]
                + [whole(piece)] * half
                + [pl.BlockSpec(memory_space=pl.ANY)] * len(filled),
                out_specs=pl.BlockSpec(
                    (half, slots, width), lambda i, me_ref: (me_ref[0] // half ^ flip, 0, 0)
                ),
                scratch_shapes=[pltpu.VMEM((count // 2, width), BF16)],
            ),
            input_output_aliases={4 + half: 0} if filled else {},
            compiler_params=pltpu.CompilerParams(vmem_limit_bytes=VMEM_BYTES),
            cost_estimate=pl.CostEstimate(
                flops=3 * flops // 2, bytes_accessed=6 * width * hidden, transcendentals=0
            ),
            name=name,
        )(me, *mats, *pieces, *filled)

    outs = forward_of(fown, 0, "forward_own")
    outs = forward_of(ffar, 1, "forward_far", outs)
    outs = exchange(after(outs, grads, gate_wgrad, up_wgrad, down_wgrad, packed), "outs")
    cuts = 4 if experts % 4 == 0 else 1

    def full(array):
        return pl.BlockSpec(array.shape, lambda i: (0,) * len(array.shape))

    def cut_at(c):
        return pl.BlockSpec((experts // cuts, slots, width), lambda i: (c, 0, 0))

    known = [hot, xp, dy_in, gain_row]
    (grad_in,) = call(
        source_kernel,
        "source",
        [block],
        known + [grads] * cuts,
        grid=(1,),
        in_specs=[full(a) for a in known] + [cut_at(c) for c in range(cuts)],
        out_specs=[full(block)],
    )
    sums = swap([after(packed, grads)] * half, "sums")
    while len(sums) > 1:
        sums = [a + b for a, b in zip(sums[::2], sums[1::2])]
    sums = sums[0] + hop(after(sums[0], grad_in), 0, half, "sums_far")
    outs = after(outs, grad_in)
    forward = (x_in.astype(F32) + dot(spread, outs.reshape(count, width))).astype(BF16)
    return (
        forward[None],
        grad_in[None],
        gate_wgrad[None, None],
        up_wgrad[None, None],
        down_wgrad[None, None],
        sums[:, :width].T[None],
        sums[:, width:].reshape(1, width),
    )


def solution(mesh):
    rows = P("pipe", "expert", None)
    weights = P("pipe", "expert", None, None)
    shared = P("pipe", None, None)
    return jax.shard_map(
        per_device,
        mesh=mesh,
        in_specs=(rows,) * 3
        + (weights,) * 3
        + (shared, P("pipe", None), rows, rows, P("pipe", "expert"), P("pipe", "expert")),
        out_specs=(rows, rows, weights, weights, weights, shared, P("pipe", None)),
        check_vma=False,
    )
```

```python
import functools

import jax
import jax.numpy as jnp
from jax import lax
from jax.experimental import pallas as pl
from jax.experimental.pallas import tpu as pltpu
from jax.sharding import PartitionSpec as P

EPS = 1e-06
F32 = jnp.float32
BF16 = jnp.bfloat16
VMEM_BYTES = 56 * 1024 * 1024
SMALL_BYTES = 24 * 1024 * 1024
LANES = 128
SCALE = 64


def hop(block, pipe_step, flip, name):
    pipes, experts = lax.axis_size("pipe"), lax.axis_size("expert")
    with jax.named_scope(name):
        if pipe_step == 0:
            return lax.ppermute(block, "expert", [(e, e ^ flip) for e in range(experts)])
        route = [
            (p * experts + e, ((p + pipe_step) % pipes) * experts + (e ^ flip))
            for p in range(pipes)
            for e in range(experts)
        ]
        return lax.ppermute(block, ("pipe", "expert"), route)


def after(block, *earlier):
    return lax.optimization_barrier((block,) + earlier)[0]


def dot(a, b):
    return jnp.dot(a, b, preferred_element_type=F32)


def dot_t(a, b):
    return lax.dot_general(a, b, (((1,), (1,)), ((), ())), preferred_element_type=F32)


def t_dot(a, b, precision=None):
    dims = (((0,), (0,)), ((), ()))
    return lax.dot_general(a, b, dims, preferred_element_type=F32, precision=precision)


def iota(shape, dim):
    return lax.broadcasted_iota(jnp.int32, shape, dim)


def call(kernel, name, outs, ins, grid=(), in_specs=None, out_specs=None, scratch=(), flops=0, limit=SMALL_BYTES):
    whole = pl.BlockSpec(memory_space=pltpu.VMEM)
    moved = sum(a.size * a.dtype.itemsize for a in list(outs) + list(ins))
    return pl.pallas_call(
        kernel,
        out_shape=[jax.ShapeDtypeStruct(o.shape, o.dtype) for o in outs],
        grid=grid,
        in_specs=in_specs or [whole] * len(ins),
        out_specs=out_specs or [whole] * len(outs),
        scratch_shapes=list(scratch),
        compiler_params=pltpu.CompilerParams(vmem_limit_bytes=limit),
        cost_estimate=pl.CostEstimate(flops=flops // SCALE, bytes_accessed=moved // SCALE, transcendentals=0),
        name=name,
    )(*ins)


def shape(dims, dtype=BF16):
    return jax.ShapeDtypeStruct(tuple(dims), dtype)


def rank_kernel(capacity, top, table_ref, *rank_refs):
    experts, tokens = rank_refs[0].shape
    for batch, rank_ref in enumerate(rank_refs):
        row = 2 * top + batch
        order = jnp.broadcast_to(table_ref[row : row + 1, :], (tokens, tokens))
        before = (order.T < order).astype(F32).astype(BF16)
        chosen = iota((experts, tokens), 0) < 0
        for routes in route_rows(table_ref, batch, top):
            chosen = chosen | (routes == iota((experts, tokens), 0))
        count = dot(chosen.astype(F32).astype(BF16), before)
        rank_ref[...] = jnp.where(chosen & (count < capacity), count.astype(jnp.int32), -1)


def route_rows(ref, batch, top):
    return [ref[batch * top + j : batch * top + j + 1, :] for j in range(top)]


def slot_mask(rank_ref, e, slots):
    rank = rank_ref[e : e + 1, :]
    return iota((slots, rank.shape[1]), 0) == rank


def one_hot(mask):
    return jnp.where(mask, 1.0, 0.0).astype(BF16)


def normalise(x_ref, gain_ref, normed_ref, step=32):
    def part(i, carry):
        rows = pl.ds(pl.multiple_of(i * step, step), step)
        values = x_ref[rows, :].astype(F32)
        scale = lax.rsqrt(jnp.mean(values * values, axis=-1, keepdims=True) + EPS)
        normed_ref[rows, :] = (values * scale * gain_ref[...]).astype(BF16)
        return carry

    lax.fori_loop(0, x_ref.shape[0] // step, part, 0)


def sigmoids(normed_ref, router_ref, routes):
    logits = dot_t(router_ref[...], normed_ref[...])
    everyone = iota(logits.shape, 0)
    picked = [jnp.sum(jnp.where(r == everyone, logits, 0.0), axis=0, keepdims=True) for r in routes]
    return [jax.nn.sigmoid(value) for value in picked]


def side_of(expert, experts, routes, lifted):
    tokens = routes[0].shape[1]
    everyone = iota((experts, tokens), 0)
    total = functools.reduce(jnp.add, lifted)
    slope = jnp.zeros((experts, tokens), F32)
    mine = jnp.zeros((1, tokens), F32)
    for r, value in zip(routes, lifted):
        slope = slope + jnp.where(r == everyone, value * (1.0 - value), 0.0)
        mine = mine + jnp.where(r == expert, value, 0.0)
    acts = slope * (jnp.where(everyone == expert, 1.0 / total, 0.0) - mine / (total * total))
    high = acts.astype(BF16).astype(F32)
    weight = jnp.broadcast_to(mine / total, (LANES - 2 * experts, tokens))
    return jnp.concatenate([high, acts - high, weight], axis=0).astype(BF16)


def put_pieces(me_ref, rank_ref, block_ref, pieces, routes=None, lifted=None):
    width = block_ref.shape[1]
    for k, piece in enumerate(pieces):
        expert = me_ref[0] ^ k
        rank = rank_ref[pl.ds(expert, 1), :]
        hot = one_hot(iota((piece.shape[0], rank.shape[1]), 0) == rank)
        piece[:, :width] = dot(hot, block_ref[...]).astype(BF16)
        if lifted:
            side = side_of(expert, rank_ref.shape[0], routes, lifted)
            piece[:, width:] = dot_t(hot, side).astype(BF16)


def back_rows_kernel(half, top, *refs):
    me_ref, x_ref, gain_ref, router_ref, table_ref, rank_ref = refs[:6]
    pieces, normed_ref = refs[6:-1], refs[-1]
    normalise(x_ref, gain_ref, normed_ref)
    routes = route_rows(table_ref, 1, top)
    lifted = sigmoids(normed_ref, router_ref, routes)
    put_pieces(me_ref, rank_ref, normed_ref, pieces, routes, lifted)


def next_rows_kernel(half, top, *refs):
    me_ref, x_ref, gain_ref, router_ref, table_ref, rank_ref = refs[:6]
    pieces, weight_ref, normed_ref = refs[6 : 6 + half], refs[6 + half], refs[-1]
    normalise(x_ref, gain_ref, normed_ref)
    put_pieces(me_ref, rank_ref, normed_ref, pieces)
    routes = route_rows(table_ref, 0, top)
    lifted = sigmoids(normed_ref, router_ref, routes)
    total = functools.reduce(jnp.add, lifted)
    weight = jnp.zeros(weight_ref.shape, F32)
    for r, value in zip(routes, lifted):
        weight = weight + jnp.where(r == iota(weight.shape, 0), value / total, 0.0)
    weight_ref[...] = weight


def cots_kernel(rank_ref, x_ref, message_ref):
    for e in range(message_ref.shape[0]):
        hot = one_hot(slot_mask(rank_ref, e, message_ref.shape[1]))
        message_ref[e] = dot(hot, x_ref[...]).astype(BF16)


def flat_of(ref):
    return ref[...].reshape(-1, ref.shape[-1])


def each_sender(me_ref, count, slots):
    for k in range(count):
        sender = me_ref[0] ^ k
        yield k, sender, pl.ds(pl.multiple_of(sender * slots, 16), slots)


def expert_kernel(steps, blocks, half, *refs):
    me_ref, gate_a, up_a, down_a, gate_b, up_b, down_b, router_ref, gain_ref, cot_ref = refs[:10]
    pieces, refs = refs[10 : 10 + 2 * half], refs[10 + 2 * half :]
    message_ref, rows_ref, scaled_ref, active_ref, gate_part_ref, up_part_ref, sums_ref = refs[:7]
    side_ref, inner_ref, high_ref, low_ref = refs[7:]
    slots, columns, part = pieces[0].shape[0], gate_b.shape[0], gate_a.shape[1]
    count, width = rows_ref.shape
    experts = router_ref.shape[0]
    step = pl.program_id(0)

    def span_of(first):
        return pl.ds(pl.multiple_of((step - first) * columns, 128), columns)

    @pl.when(step == 0)
    def _():
        for k, sender, rows in each_sender(me_ref, 2 * half, slots):
            rows_ref[rows, :] = pieces[k][:, :width]
            side = pieces[k][:, width:]
            side_ref[rows, :] = side
            scale = side.astype(F32)[:, LANES - 1 :]
            scaled_ref[rows, :] = (scale * cot_ref[sender].astype(F32)).astype(BF16)
        inner_ref[...] = jnp.zeros_like(inner_ref)
        sums_ref[...] = jnp.zeros_like(sums_ref)

    @pl.when(step < steps)
    def _():
        gate = dot(rows_ref[...], gate_a[...])
        upper = dot(rows_ref[...], up_a[...])
        sig = jax.nn.sigmoid(gate)
        act_grad = dot_t(scaled_ref[...], down_a[...])
        active_ref[step] = (gate * sig * upper).astype(BF16)
        gate_part_ref[step] = (act_grad * upper * sig * (1.0 + gate * (1.0 - sig))).astype(BF16)
        up_part_ref[step] = (act_grad * (gate * sig)).astype(BF16)

    @pl.when((step >= steps) & (step < steps + blocks))
    def _():
        result = jnp.zeros((count, columns), F32)
        for f in range(steps):
            result = result + dot(active_ref[f], down_b[f * part : (f + 1) * part, :])
        cot = cot_ref[:, :, span_of(steps)].reshape(count, columns).astype(F32)
        result = result.astype(BF16).astype(F32)
        inner_ref[...] += jnp.sum(cot * result, axis=1, keepdims=True)

    @pl.when(step == steps + blocks)
    def _():
        terms = inner_ref[...].astype(BF16).astype(F32) * side_ref[...].astype(F32)
        high_ref[...] = terms.astype(BF16)
        low_ref[...] = (terms - terms.astype(BF16).astype(F32)).astype(BF16)

    @pl.when(step >= steps + blocks)
    def _():
        span = span_of(steps + blocks)
        rows = rows_ref[:, span]
        router = router_ref[:, span].astype(F32)
        rest = jnp.zeros((LANES - 2 * experts, columns), F32)
        router = jnp.concatenate([router, router, rest], axis=0).astype(BF16)
        total = dot(high_ref[...], router) + dot(low_ref[...], router)
        for f in range(steps):
            units = slice(f * part, (f + 1) * part)
            total = total + dot_t(gate_part_ref[f], gate_b[:, units])
            total = total + dot_t(up_part_ref[f], up_b[:, units])
        message_ref[:, span] = total.astype(BF16)
        terms = t_dot(high_ref[...], rows) + t_dot(low_ref[...], rows)
        sums_ref[:experts, span] = terms[:experts] + terms[experts : 2 * experts]
        gain_sum = jnp.sum(total * rows.astype(F32), axis=0, keepdims=True)
        sums_ref[experts : experts + 1, span] = gain_sum / gain_ref[:, span]


def forward_kernel(half, flip, me_ref, gate_w, up_w, down_w, *refs):
    pieces, (out_ref, rows_ref) = refs[:half], refs[-2:]
    slots = pieces[0].shape[0]
    for k, piece in enumerate(pieces):
        start = pl.multiple_of((me_ref[0] ^ k) % half * slots, 16)
        rows_ref[pl.ds(start, slots), :] = piece[...]
    gate = dot(rows_ref[...], gate_w[...])
    active = (gate * jax.nn.sigmoid(gate) * dot(rows_ref[...], up_w[...])).astype(BF16)
    columns = 512 if out_ref.shape[2] % 512 == 0 else out_ref.shape[2]
    for c in range(0, out_ref.shape[2], columns):
        result = dot(active, down_w[:, c : c + columns]).astype(BF16)
        senders = pl.ds((me_ref[0] // half ^ flip) * half, half)
        out_ref[senders, :, c : c + columns] = result.reshape(half, slots, columns)


def spread_kernel(slots, rank_ref, weight_ref, spread_ref, flat_ref):
    for e in range(rank_ref.shape[0]):
        mask = slot_mask(rank_ref, e, slots)
        flat_ref[e * slots : (e + 1) * slots, :] = jnp.where(mask, weight_ref[e : e + 1, :], 0.0)
    spread_ref[...] = flat_ref[...].T.astype(BF16)


def source_kernel(hot_ref, xp_ref, dy_ref, gain_ref, *refs):
    grads, grad_ref = refs[:-1], refs[-1]
    dnormed = jnp.zeros(xp_ref.shape, F32)
    for c, ref in enumerate(grads):
        rows = flat_of(ref)
        part = slice(c * rows.shape[0], (c + 1) * rows.shape[0])
        dnormed = dnormed + dot(hot_ref[:, part], rows)
    values = xp_ref[...].astype(F32)
    scale = lax.rsqrt(jnp.mean(values * values, axis=-1, keepdims=True) + EPS)
    bare = values * scale
    lifted_grad = dnormed * gain_ref[...]
    slope = jnp.mean(lifted_grad * bare, axis=-1, keepdims=True)
    grad_ref[...] = (dy_ref[...].astype(F32) + scale * (lifted_grad - bare * slope)).astype(BF16)


def per_device(
    next_input,
    prev_input,
    next_cot,
    gate_weight,
    up_weight,
    down_weight,
    router,
    gain,
    next_routes,
    prev_routes,
    next_priority,
    prev_priority,
):
    experts = router.shape[-1]
    tokens, width = next_input.shape[1:]
    hidden = gate_weight.shape[-1]
    top = next_routes.shape[-1]
    capacity = (5 * top * tokens + 4 * experts - 1) // (4 * experts)
    slots = -(-capacity // 16) * 16
    mats = [gate_weight[0, 0], up_weight[0, 0], down_weight[0, 0]]
    gain_row, router_t = (gain, router[0].T)
    partial = functools.partial
    block, message = shape((tokens, width)), shape((experts, slots, width))
    per_token = shape((experts, tokens), F32)

    def exchange(array, name, groups=None):
        with jax.named_scope(name):
            return lax.all_to_all(array, "expert", 0, 0, tiled=True, axis_index_groups=groups)

    def swap(pieces, name):
        return [piece if k == 0 else hop(piece, 0, k, name) for k, piece in enumerate(pieces)]

    half = lax.axis_size("expert") // 2
    me = lax.axis_index("expert").astype(jnp.int32).reshape(1)
    smem, vmem = pl.BlockSpec(memory_space=pltpu.SMEM), pl.BlockSpec(memory_space=pltpu.VMEM)
    xp = prev_input[0]
    xp_far = hop(xp, 0, half, "xp_far")
    dy_in = hop(next_cot[0], -1, 0, "dy_in")
    x_in = hop(next_input[0], 1, 0, "x_in")
    table = jnp.concatenate(
        [next_routes[0].T, prev_routes[0].T, next_priority, prev_priority], axis=0
    )
    far_table = hop(table, 0, half, "tables")

    def ranks(table, name):
        dims = shape((experts, tokens), jnp.int32)
        return call(partial(rank_kernel, capacity, top), name, [dims] * 2, [table])

    frank, rank = ranks(table, "ranks")
    piece, normed_scratch = shape((slots, width)), pltpu.VMEM((tokens, width), BF16)
    frank_far, rank_far = ranks(far_table, "far_ranks")
    longer_piece = shape((slots, width + LANES))

    def back_rows(x, table, rank, name):
        pieces = call(
            partial(back_rows_kernel, half, top),
            name,
            [longer_piece] * half,
            [me, x, gain_row, router_t, table, rank],
            in_specs=[smem] + [vmem] * 5,
            scratch=[normed_scratch],
        )
        return swap(pieces, name)

    def next_rows(x, table, rank, name):
        outs = call(
            partial(next_rows_kernel, half, top),
            name,
            [piece] * half + [per_token],
            [me, x, gain_row, router_t, table, rank],
            in_specs=[smem] + [vmem] * 5,
            scratch=[normed_scratch],
        )
        return swap(outs[:half], name), outs[0], outs[half]

    own = back_rows(xp, table, rank, "own_rows")
    (cots,) = call(cots_kernel, "cots", [message], [rank, dy_in])
    cots = exchange(after(cots, xp_far, far_table, *own[1:]), "cots")
    far = back_rows(xp_far, far_table, rank_far, "far_rows")
    x_far = hop(after(next_input[0], cots, *far[1:]), 1, half, "x_far")
    fown, _, fweight = next_rows(x_in, table, frank, "fown_rows")
    ffar, ffar_sent, _ = next_rows(x_far, far_table, frank_far, "ffar_rows")

    count = experts * slots
    part = 256 if hidden % 256 == 0 else hidden
    columns = 512 if width % 512 == 0 else width
    steps = hidden // part
    blocks = width // columns
    grid = (steps + 2 * blocks,)

    def whole(dims):
        return pl.BlockSpec(dims.shape, lambda *_: (0,) * len(dims.shape), pipeline_mode=pl.Buffered(1))

    def early(i):
        return jnp.minimum(i, steps - 1)

    def middle(i):
        return jnp.clip(i - steps, 0, blocks - 1)

    def late(i):
        return jnp.maximum(i - steps - blocks, 0)

    across_a = pl.BlockSpec((width, part), lambda i, *_: (0, early(i)))
    down_a = pl.BlockSpec((part, width), lambda i: (early(i), 0))
    across_b = pl.BlockSpec((columns, hidden), lambda i: (late(i), 0))
    down_b = pl.BlockSpec((hidden, columns), lambda i, *_: (0, middle(i)))
    flops = 2 * count * width * hidden
    def spread_of(rank, weight, name):
        return call(
            partial(spread_kernel, slots),
            name,
            [shape((tokens, count))],
            [rank, weight],
            scratch=[pltpu.VMEM((count, tokens), F32)],
        )[0]

    spread = spread_of(frank, fweight, "spread")
    hot = spread_of(rank, jnp.ones((experts, tokens), F32), "hot")
    flat, hidden_shape = shape((count, width)), shape((steps, count, part))
    sums_shape = shape((-(-(experts + 1) // 8) * 8, width), F32)
    grads, flat_rows, scaled, active, gate_part, up_part, sums = call(
        partial(expert_kernel, steps, blocks, half),
        "expert",
        [flat] * 3 + [hidden_shape] * 3 + [sums_shape],
        [me] + mats + mats + [router_t, gain_row, cots] + own + far,
        grid=grid,
        in_specs=[smem, across_a, across_a, down_a, across_b, across_b, down_b]
        + [whole(router_t), whole(gain_row), whole(message)]
        + [whole(longer_piece)] * experts,
        out_specs=[whole(flat)] * 3 + [whole(hidden_shape)] * 3 + [whole(sums_shape)],
        scratch=[
            pltpu.VMEM((count, LANES), BF16),
            pltpu.VMEM((count, 1), F32),
            pltpu.VMEM((count, LANES), BF16),
            pltpu.VMEM((count, LANES), BF16),
        ],
        flops=6 * flops,
        limit=VMEM_BYTES,
    )
    active, gate_part, up_part = (
        jnp.swapaxes(a, 0, 1).reshape(count, hidden) for a in (active, gate_part, up_part)
    )
    grads = grads.reshape(experts, slots, width)
    grads = exchange(after(grads, x_far, hot, spread, *fown[1:]), "grads")
    flat_rows, active = after((flat_rows, active), ffar_sent)
    gate_wgrad = t_dot(flat_rows, gate_part).astype(BF16)
    up_wgrad = t_dot(flat_rows, up_part).astype(BF16)
    down_wgrad = t_dot(active, scaled).astype(BF16)
    packed = [sums[:experts], sums[experts].reshape(experts, width // experts)]
    packed = jnp.concatenate(packed, axis=1)

    def forward_of(pieces, flip, name, *filled):
        return pl.pallas_call(
            partial(forward_kernel, half, flip),
            out_shape=message,
            in_specs=[smem] + [vmem] * (3 + half + len(filled)),
            out_specs=vmem,
            scratch_shapes=[pltpu.VMEM((count // 2, width), BF16)],
            input_output_aliases={4 + half: 0} if filled else {},
            compiler_params=pltpu.CompilerParams(vmem_limit_bytes=SMALL_BYTES),
            cost_estimate=pl.CostEstimate(
                flops=3 * flops // 2, bytes_accessed=6 * width * hidden, transcendentals=0
            ),
            name=name,
        )(me, *mats, *pieces, *filled)

    outs = forward_of(fown, 0, "forward_own")
    outs = forward_of(ffar, 1, "forward_far", outs)
    outs = exchange(after(outs, grads, gate_wgrad, up_wgrad, down_wgrad, packed), "outs")
    cuts = 4 if experts % 4 == 0 else 1

    def full(array):
        return pl.BlockSpec(array.shape, lambda i: (0,) * len(array.shape))

    def cut_at(c):
        return pl.BlockSpec((experts // cuts, slots, width), lambda i: (c, 0, 0))

    known = [hot, xp, dy_in, gain_row]
    (grad_in,) = call(
        source_kernel,
        "source",
        [block],
        known + [grads] * cuts,
        grid=(1,),
        in_specs=[full(a) for a in known] + [cut_at(c) for c in range(cuts)],
        out_specs=[full(block)],
    )
    sums = swap([after(packed, grads)] * half, "sums")
    while len(sums) > 1:
        sums = [a + b for a, b in zip(sums[::2], sums[1::2])]
    sums = sums[0] + hop(after(sums[0], grad_in), 0, half, "sums_far")
    outs = after(outs, grad_in)
    forward = (x_in.astype(F32) + dot(spread, outs.reshape(count, width))).astype(BF16)
    return (
        forward[None],
        grad_in[None],
        gate_wgrad[None, None],
        up_wgrad[None, None],
        down_wgrad[None, None],
        sums[:, :width].T[None],
        sums[:, width:].reshape(1, width),
    )


def solution(mesh):
    rows = P("pipe", "expert", None)
    weights = P("pipe", "expert", None, None)
    shared = P("pipe", None, None)
    return jax.shard_map(
        per_device,
        mesh=mesh,
        in_specs=(rows,) * 3
        + (weights,) * 3
        + (shared, P("pipe", None), rows, rows, P("pipe", "expert"), P("pipe", "expert")),
        out_specs=(rows, rows, weights, weights, weights, shared, P("pipe", None)),
        check_vma=False,
    )
```

```python
import functools

import jax
import jax.numpy as jnp
from jax import lax
from jax.experimental import pallas as pl
from jax.experimental.pallas import tpu as pltpu
from jax.sharding import PartitionSpec as P

EPS = 1e-06
F32 = jnp.float32
BF16 = jnp.bfloat16
VMEM_BYTES = 56 * 1024 * 1024
SMALL_BYTES = 24 * 1024 * 1024
LANES = 128
SCALE = 64


def hop(block, pipe_step, flip, name):
    pipes, experts = lax.axis_size("pipe"), lax.axis_size("expert")
    with jax.named_scope(name):
        if pipe_step == 0:
            return lax.ppermute(block, "expert", [(e, e ^ flip) for e in range(experts)])
        route = [
            (p * experts + e, ((p + pipe_step) % pipes) * experts + (e ^ flip))
            for p in range(pipes)
            for e in range(experts)
        ]
        return lax.ppermute(block, ("pipe", "expert"), route)


def after(block, *earlier):
    return lax.optimization_barrier((block,) + earlier)[0]


def dot(a, b):
    return jnp.dot(a, b, preferred_element_type=F32)


def dot_t(a, b):
    return lax.dot_general(a, b, (((1,), (1,)), ((), ())), preferred_element_type=F32)


def t_dot(a, b, precision=None):
    dims = (((0,), (0,)), ((), ()))
    return lax.dot_general(a, b, dims, preferred_element_type=F32, precision=precision)


def iota(shape, dim):
    return lax.broadcasted_iota(jnp.int32, shape, dim)


def call(kernel, name, outs, ins, grid=(), in_specs=None, out_specs=None, scratch=(), flops=0, limit=SMALL_BYTES):
    whole = pl.BlockSpec(memory_space=pltpu.VMEM)
    moved = sum(a.size * a.dtype.itemsize for a in list(outs) + list(ins))
    return pl.pallas_call(
        kernel,
        out_shape=[jax.ShapeDtypeStruct(o.shape, o.dtype) for o in outs],
        grid=grid,
        in_specs=in_specs or [whole] * len(ins),
        out_specs=out_specs or [whole] * len(outs),
        scratch_shapes=list(scratch),
        compiler_params=pltpu.CompilerParams(vmem_limit_bytes=limit),
        cost_estimate=pl.CostEstimate(flops=flops // SCALE, bytes_accessed=moved // SCALE, transcendentals=0),
        name=name,
    )(*ins)


def shape(dims, dtype=BF16):
    return jax.ShapeDtypeStruct(tuple(dims), dtype)


def rank_kernel(capacity, top, table_ref, *rank_refs):
    experts, tokens = rank_refs[0].shape
    for batch, rank_ref in enumerate(rank_refs):
        row = 2 * top + batch
        order = jnp.broadcast_to(table_ref[row : row + 1, :], (tokens, tokens))
        before = (order.T < order).astype(F32).astype(BF16)
        chosen = iota((experts, tokens), 0) < 0
        for routes in route_rows(table_ref, batch, top):
            chosen = chosen | (routes == iota((experts, tokens), 0))
        count = dot(chosen.astype(F32).astype(BF16), before)
        rank_ref[...] = jnp.where(chosen & (count < capacity), count.astype(jnp.int32), -1)


def route_rows(ref, batch, top):
    return [ref[batch * top + j : batch * top + j + 1, :] for j in range(top)]


def slot_mask(rank_ref, e, slots):
    rank = rank_ref[e : e + 1, :]
    return iota((slots, rank.shape[1]), 0) == rank


def one_hot(mask):
    return jnp.where(mask, 1.0, 0.0).astype(BF16)


def normalise(x_ref, gain_ref, normed_ref, step=32):
    def part(i, carry):
        rows = pl.ds(pl.multiple_of(i * step, step), step)
        values = x_ref[rows, :].astype(F32)
        scale = lax.rsqrt(jnp.mean(values * values, axis=-1, keepdims=True) + EPS)
        normed_ref[rows, :] = (values * scale * gain_ref[...]).astype(BF16)
        return carry

    lax.fori_loop(0, x_ref.shape[0] // step, part, 0)


def sigmoids(normed_ref, router_ref, routes):
    logits = dot_t(router_ref[...], normed_ref[...])
    everyone = iota(logits.shape, 0)
    picked = [jnp.sum(jnp.where(r == everyone, logits, 0.0), axis=0, keepdims=True) for r in routes]
    return [jax.nn.sigmoid(value) for value in picked]


def side_of(expert, experts, routes, lifted):
    tokens = routes[0].shape[1]
    everyone = iota((experts, tokens), 0)
    total = functools.reduce(jnp.add, lifted)
    slope = jnp.zeros((experts, tokens), F32)
    mine = jnp.zeros((1, tokens), F32)
    for r, value in zip(routes, lifted):
        slope = slope + jnp.where(r == everyone, value * (1.0 - value), 0.0)
        mine = mine + jnp.where(r == expert, value, 0.0)
    acts = slope * (jnp.where(everyone == expert, 1.0 / total, 0.0) - mine / (total * total))
    high = acts.astype(BF16).astype(F32)
    weight = jnp.broadcast_to(mine / total, (LANES - 2 * experts, tokens))
    return jnp.concatenate([high, acts - high, weight], axis=0).astype(BF16)


def put_pieces(me_ref, rank_ref, block_ref, pieces, routes=None, lifted=None):
    width = block_ref.shape[1]
    for k, piece in enumerate(pieces):
        expert = me_ref[0] ^ k
        rank = rank_ref[pl.ds(expert, 1), :]
        hot = one_hot(iota((piece.shape[0], rank.shape[1]), 0) == rank)
        piece[:, :width] = dot(hot, block_ref[...]).astype(BF16)
        if lifted:
            side = side_of(expert, rank_ref.shape[0], routes, lifted)
            piece[:, width:] = dot_t(hot, side).astype(BF16)


def back_rows_kernel(half, top, *refs):
    me_ref, x_ref, gain_ref, router_ref, table_ref, rank_ref = refs[:6]
    pieces, normed_ref = refs[6:-1], refs[-1]
    normalise(x_ref, gain_ref, normed_ref)
    routes = route_rows(table_ref, 1, top)
    lifted = sigmoids(normed_ref, router_ref, routes)
    put_pieces(me_ref, rank_ref, normed_ref, pieces, routes, lifted)


def next_rows_kernel(half, top, *refs):
    me_ref, x_ref, gain_ref, router_ref, table_ref, rank_ref = refs[:6]
    pieces, weight_ref, normed_ref = refs[6 : 6 + half], refs[6 + half], refs[-1]
    normalise(x_ref, gain_ref, normed_ref)
    put_pieces(me_ref, rank_ref, normed_ref, pieces)
    routes = route_rows(table_ref, 0, top)
    lifted = sigmoids(normed_ref, router_ref, routes)
    total = functools.reduce(jnp.add, lifted)
    weight = jnp.zeros(weight_ref.shape, F32)
    for r, value in zip(routes, lifted):
        weight = weight + jnp.where(r == iota(weight.shape, 0), value / total, 0.0)
    weight_ref[...] = weight


def cots_kernel(rank_ref, x_ref, message_ref):
    for e in range(message_ref.shape[0]):
        hot = one_hot(slot_mask(rank_ref, e, message_ref.shape[1]))
        message_ref[e] = dot(hot, x_ref[...]).astype(BF16)


def flat_of(ref):
    return ref[...].reshape(-1, ref.shape[-1])


def each_sender(me_ref, count, slots):
    for k in range(count):
        sender = me_ref[0] ^ k
        yield k, sender, pl.ds(pl.multiple_of(sender * slots, 16), slots)


def expert_kernel(steps, blocks, half, *refs):
    me_ref, gate_a, up_a, down_a, gate_b, up_b, down_b, router_ref, gain_ref, cot_ref = refs[:10]
    pieces, refs = refs[10 : 10 + 2 * half], refs[10 + 2 * half :]
    message_ref, rows_ref, scaled_ref, active_ref, gate_part_ref, up_part_ref, sums_ref = refs[:7]
    side_ref, inner_ref, high_ref, low_ref = refs[7:]
    slots, columns, part = pieces[0].shape[0], gate_b.shape[0], gate_a.shape[1]
    count, width = rows_ref.shape
    experts = router_ref.shape[0]
    step = pl.program_id(0)

    def span_of(first):
        return pl.ds(pl.multiple_of((step - first) * columns, 128), columns)

    @pl.when(step == 0)
    def _():
        for k, sender, rows in each_sender(me_ref, 2 * half, slots):
            rows_ref[rows, :] = pieces[k][:, :width]
            side = pieces[k][:, width:]
            side_ref[rows, :] = side
            scale = side.astype(F32)[:, LANES - 1 :]
            scaled_ref[rows, :] = (scale * cot_ref[sender].astype(F32)).astype(BF16)
        inner_ref[...] = jnp.zeros_like(inner_ref)
        sums_ref[...] = jnp.zeros_like(sums_ref)

    @pl.when(step < steps)
    def _():
        gate = dot(rows_ref[...], gate_a[...])
        upper = dot(rows_ref[...], up_a[...])
        sig = jax.nn.sigmoid(gate)
        act_grad = dot_t(scaled_ref[...], down_a[...])
        active_ref[step] = (gate * sig * upper).astype(BF16)
        gate_part_ref[step] = (act_grad * upper * sig * (1.0 + gate * (1.0 - sig))).astype(BF16)
        up_part_ref[step] = (act_grad * (gate * sig)).astype(BF16)

    @pl.when((step >= steps) & (step < steps + blocks))
    def _():
        result = jnp.zeros((count, columns), F32)
        for f in range(steps):
            result = result + dot(active_ref[f], down_b[f * part : (f + 1) * part, :])
        cot = cot_ref[:, :, span_of(steps)].reshape(count, columns).astype(F32)
        result = result.astype(BF16).astype(F32)
        inner_ref[...] += jnp.sum(cot * result, axis=1, keepdims=True)

    @pl.when(step == steps + blocks)
    def _():
        terms = inner_ref[...].astype(BF16).astype(F32) * side_ref[...].astype(F32)
        high_ref[...] = terms.astype(BF16)
        low_ref[...] = (terms - terms.astype(BF16).astype(F32)).astype(BF16)

    @pl.when(step >= steps + blocks)
    def _():
        span = span_of(steps + blocks)
        rows = rows_ref[:, span]
        router = router_ref[:, span].astype(F32)
        rest = jnp.zeros((LANES - 2 * experts, columns), F32)
        router = jnp.concatenate([router, router, rest], axis=0).astype(BF16)
        total = dot(high_ref[...], router) + dot(low_ref[...], router)
        for f in range(steps):
            units = slice(f * part, (f + 1) * part)
            total = total + dot_t(gate_part_ref[f], gate_b[:, units])
            total = total + dot_t(up_part_ref[f], up_b[:, units])
        message_ref[:, span] = total.astype(BF16)
        terms = t_dot(high_ref[...], rows) + t_dot(low_ref[...], rows)
        sums_ref[:experts, span] = terms[:experts] + terms[experts : 2 * experts]
        gain_sum = jnp.sum(total * rows.astype(F32), axis=0, keepdims=True)
        sums_ref[experts : experts + 1, span] = gain_sum / gain_ref[:, span]


def forward_kernel(half, flip, me_ref, gate_w, up_w, down_w, *refs):
    pieces, (out_ref, rows_ref) = refs[:half], refs[-2:]
    slots = pieces[0].shape[0]
    for k, piece in enumerate(pieces):
        start = pl.multiple_of((me_ref[0] ^ k) % half * slots, 16)
        rows_ref[pl.ds(start, slots), :] = piece[...]
    gate = dot(rows_ref[...], gate_w[...])
    active = (gate * jax.nn.sigmoid(gate) * dot(rows_ref[...], up_w[...])).astype(BF16)
    columns = 512 if out_ref.shape[2] % 512 == 0 else out_ref.shape[2]
    for c in range(0, out_ref.shape[2], columns):
        result = dot(active, down_w[:, c : c + columns]).astype(BF16)
        senders = pl.ds((me_ref[0] // half ^ flip) * half, half)
        out_ref[senders, :, c : c + columns] = result.reshape(half, slots, columns)


def spread_kernel(slots, rank_ref, weight_ref, spread_ref, flat_ref):
    for e in range(rank_ref.shape[0]):
        mask = slot_mask(rank_ref, e, slots)
        flat_ref[e * slots : (e + 1) * slots, :] = jnp.where(mask, weight_ref[e : e + 1, :], 0.0)
    spread_ref[...] = flat_ref[...].T.astype(BF16)


def source_kernel(hot_ref, xp_ref, dy_ref, gain_ref, *refs):
    grads, grad_ref = refs[:-1], refs[-1]
    dnormed = jnp.zeros(xp_ref.shape, F32)
    for c, ref in enumerate(grads):
        rows = flat_of(ref)
        part = slice(c * rows.shape[0], (c + 1) * rows.shape[0])
        dnormed = dnormed + dot(hot_ref[:, part], rows)
    values = xp_ref[...].astype(F32)
    scale = lax.rsqrt(jnp.mean(values * values, axis=-1, keepdims=True) + EPS)
    bare = values * scale
    lifted_grad = dnormed * gain_ref[...]
    slope = jnp.mean(lifted_grad * bare, axis=-1, keepdims=True)
    grad_ref[...] = (dy_ref[...].astype(F32) + scale * (lifted_grad - bare * slope)).astype(BF16)


def per_device(
    next_input,
    prev_input,
    next_cot,
    gate_weight,
    up_weight,
    down_weight,
    router,
    gain,
    next_routes,
    prev_routes,
    next_priority,
    prev_priority,
):
    experts = router.shape[-1]
    tokens, width = next_input.shape[1:]
    hidden = gate_weight.shape[-1]
    top = next_routes.shape[-1]
    capacity = (5 * top * tokens + 4 * experts - 1) // (4 * experts)
    slots = -(-capacity // 16) * 16
    mats = [gate_weight[0, 0], up_weight[0, 0], down_weight[0, 0]]
    gain_row, router_t = (gain, router[0].T)
    partial = functools.partial
    block, message = shape((tokens, width)), shape((experts, slots, width))
    per_token = shape((experts, tokens), F32)

    def exchange(array, name, groups=None):
        with jax.named_scope(name):
            return lax.all_to_all(array, "expert", 0, 0, tiled=True, axis_index_groups=groups)

    def swap(pieces, name):
        return [piece if k == 0 else hop(piece, 0, k, name) for k, piece in enumerate(pieces)]

    half = lax.axis_size("expert") // 2
    me = lax.axis_index("expert").astype(jnp.int32).reshape(1)
    smem, vmem = pl.BlockSpec(memory_space=pltpu.SMEM), pl.BlockSpec(memory_space=pltpu.VMEM)
    xp = prev_input[0]
    xp_far = hop(xp, 0, half, "xp_far")
    table = jnp.concatenate(
        [next_routes[0].T, prev_routes[0].T, next_priority, prev_priority], axis=0
    )
    far_table = hop(table, 0, half, "tables")
    dy_in = hop(after(next_cot[0], table), -1, 0, "dy_in")
    x_in = hop(after(next_input[0], xp_far), 1, 0, "x_in")

    def ranks(table, name):
        dims = shape((experts, tokens), jnp.int32)
        return call(partial(rank_kernel, capacity, top), name, [dims] * 2, [table])

    frank, rank = ranks(table, "ranks")
    piece, normed_scratch = shape((slots, width)), pltpu.VMEM((tokens, width), BF16)
    frank_far, rank_far = ranks(far_table, "far_ranks")
    longer_piece = shape((slots, width + LANES))

    def back_rows(x, table, rank, name):
        pieces = call(
            partial(back_rows_kernel, half, top),
            name,
            [longer_piece] * half,
            [me, x, gain_row, router_t, table, rank],
            in_specs=[smem] + [vmem] * 5,
            scratch=[normed_scratch],
        )
        return swap(pieces, name)

    def next_rows(x, table, rank, name):
        outs = call(
            partial(next_rows_kernel, half, top),
            name,
            [piece] * half + [per_token],
            [me, x, gain_row, router_t, table, rank],
            in_specs=[smem] + [vmem] * 5,
            scratch=[normed_scratch],
        )
        return swap(outs[:half], name), outs[0], outs[half]

    own = back_rows(xp, table, rank, "own_rows")
    (cots,) = call(cots_kernel, "cots", [message], [rank, dy_in])
    cots = exchange(after(cots, xp_far, far_table, *own[1:]), "cots")
    far = back_rows(xp_far, far_table, rank_far, "far_rows")
    x_far = hop(after(next_input[0], cots, *far[1:]), 1, half, "x_far")
    fown, _, fweight = next_rows(x_in, table, frank, "fown_rows")
    ffar, ffar_sent, _ = next_rows(x_far, far_table, frank_far, "ffar_rows")

    count = experts * slots
    part = 256 if hidden % 256 == 0 else hidden
    columns = 512 if width % 512 == 0 else width
    steps = hidden // part
    blocks = width // columns
    grid = (steps + 2 * blocks,)

    def whole(dims):
        return pl.BlockSpec(dims.shape, lambda *_: (0,) * len(dims.shape), pipeline_mode=pl.Buffered(1))

    def early(i):
        return jnp.minimum(i, steps - 1)

    def middle(i):
        return jnp.clip(i - steps, 0, blocks - 1)

    def late(i):
        return jnp.maximum(i - steps - blocks, 0)

    across_a = pl.BlockSpec((width, part), lambda i, *_: (0, early(i)))
    down_a = pl.BlockSpec((part, width), lambda i: (early(i), 0))
    across_b = pl.BlockSpec((columns, hidden), lambda i: (late(i), 0))
    down_b = pl.BlockSpec((hidden, columns), lambda i, *_: (0, middle(i)))
    flops = 2 * count * width * hidden
    def spread_of(rank, weight, name):
        return call(
            partial(spread_kernel, slots),
            name,
            [shape((tokens, count))],
            [rank, weight],
            scratch=[pltpu.VMEM((count, tokens), F32)],
        )[0]

    spread = spread_of(frank, fweight, "spread")
    hot = spread_of(rank, jnp.ones((experts, tokens), F32), "hot")
    flat, hidden_shape = shape((count, width)), shape((steps, count, part))
    sums_shape = shape((-(-(experts + 1) // 8) * 8, width), F32)
    grads, flat_rows, scaled, active, gate_part, up_part, sums = call(
        partial(expert_kernel, steps, blocks, half),
        "expert",
        [flat] * 3 + [hidden_shape] * 3 + [sums_shape],
        [me] + mats + mats + [router_t, gain_row, cots] + own + far,
        grid=grid,
        in_specs=[smem, across_a, across_a, down_a, across_b, across_b, down_b]
        + [whole(router_t), whole(gain_row), whole(message)]
        + [whole(longer_piece)] * experts,
        out_specs=[whole(flat)] * 3 + [whole(hidden_shape)] * 3 + [whole(sums_shape)],
        scratch=[
            pltpu.VMEM((count, LANES), BF16),
            pltpu.VMEM((count, 1), F32),
            pltpu.VMEM((count, LANES), BF16),
            pltpu.VMEM((count, LANES), BF16),
        ],
        flops=6 * flops,
        limit=VMEM_BYTES,
    )
    active, gate_part, up_part = (
        jnp.swapaxes(a, 0, 1).reshape(count, hidden) for a in (active, gate_part, up_part)
    )
    grads = grads.reshape(experts, slots, width)
    grads = exchange(after(grads, x_far, hot, spread, *fown[1:]), "grads")
    flat_rows, active = after((flat_rows, active), ffar_sent)
    gate_wgrad = t_dot(flat_rows, gate_part).astype(BF16)
    up_wgrad = t_dot(flat_rows, up_part).astype(BF16)
    down_wgrad = t_dot(active, scaled).astype(BF16)
    packed = [sums[:experts], sums[experts].reshape(experts, width // experts)]
    packed = jnp.concatenate(packed, axis=1)

    def forward_of(pieces, flip, name, *filled):
        return pl.pallas_call(
            partial(forward_kernel, half, flip),
            out_shape=message,
            in_specs=[smem] + [vmem] * (3 + half + len(filled)),
            out_specs=vmem,
            scratch_shapes=[pltpu.VMEM((count // 2, width), BF16)],
            input_output_aliases={4 + half: 0} if filled else {},
            compiler_params=pltpu.CompilerParams(vmem_limit_bytes=SMALL_BYTES),
            cost_estimate=pl.CostEstimate(
                flops=3 * flops // 2, bytes_accessed=6 * width * hidden, transcendentals=0
            ),
            name=name,
        )(me, *mats, *pieces, *filled)

    outs = forward_of(fown, 0, "forward_own")
    outs = forward_of(ffar, 1, "forward_far", outs)
    outs = exchange(after(outs, grads, gate_wgrad, up_wgrad, down_wgrad, packed), "outs")
    cuts = 4 if experts % 4 == 0 else 1

    def full(array):
        return pl.BlockSpec(array.shape, lambda i: (0,) * len(array.shape))

    def cut_at(c):
        return pl.BlockSpec((experts // cuts, slots, width), lambda i: (c, 0, 0))

    known = [hot, xp, dy_in, gain_row]
    (grad_in,) = call(
        source_kernel,
        "source",
        [block],
        known + [grads] * cuts,
        grid=(1,),
        in_specs=[full(a) for a in known] + [cut_at(c) for c in range(cuts)],
        out_specs=[full(block)],
    )
    sums = swap([after(packed, grads)] * half, "sums")
    while len(sums) > 1:
        sums = [a + b for a, b in zip(sums[::2], sums[1::2])]
    sums = sums[0] + hop(after(sums[0], grad_in), 0, half, "sums_far")
    outs = after(outs, grad_in)
    forward = (x_in.astype(F32) + dot(spread, outs.reshape(count, width))).astype(BF16)
    return (
        forward[None],
        grad_in[None],
        gate_wgrad[None, None],
        up_wgrad[None, None],
        down_wgrad[None, None],
        sums[:, :width].T[None],
        sums[:, width:].reshape(1, width),
    )


def solution(mesh):
    rows = P("pipe", "expert", None)
    weights = P("pipe", "expert", None, None)
    shared = P("pipe", None, None)
    return jax.shard_map(
        per_device,
        mesh=mesh,
        in_specs=(rows,) * 3
        + (weights,) * 3
        + (shared, P("pipe", None), rows, rows, P("pipe", "expert"), P("pipe", "expert")),
        out_specs=(rows, rows, weights, weights, weights, shared, P("pipe", None)),
        check_vma=False,
    )
```
